256 devices in a mesh: slab: 64 (over x, z, core), ens: 4 (over y).
Axes of the slice: x: 4, y: 4, z: 8, core: 2. Of those that a mesh axis runs over, the one named last changes fastest.
Arguments:
- field: bfloat16 [4, 64, 32, 128, 128], P('ens', 'slab'), may hold values from -6 to 6
- weight: bfloat16 [1024, 32, 1024], P('slab'), may hold values from -4 to 4
- local_weight: bfloat16 [32, 32], replicated, may hold values from -1 to 1
- bias: float32 [32], replicated, may hold values from -3 to 3
- cotangent: bfloat16 [4, 64, 32, 128, 128], P('ens', 'slab'), may hold values from -6 to 6
Outputs:
- output: bfloat16 [4, 64, 32, 128, 128], P('ens', 'slab')
- grad_field: bfloat16 [4, 64, 32, 128, 128], P('ens', 'slab')
- grad_spectral: float32 [1024, 32, 1024], P('slab')
- grad_local: float32 [32, 32], replicated
- grad_bias: float32 [32], replicated
The draws below stay inside these ranges and needn't reach their ends.
All inputs are finite; a program needn't handle non-finite values.
Results may differ from the reference program's by a relative error of at most 0.0075.
Values sent between devices are 32-bit elements; how exact they have to be, the bound alone decides.
A program may use at most 128 MiB of HBM per device.

```python
import math
import jax
import jax.numpy as jnp
from jax import lax

C = 32
NX = 128
NY = 128
K = 32
NZ = 64
MEMBERS = 4
KK = 1024


def shard_levels(key, extent, split, least, top_value):
    level, own = 1.0, jax.random.fold_in(key, 6)
    for axis_at, blocks in split:
        draws = jnp.exp(jax.random.uniform(jax.random.fold_in(own, axis_at), (blocks,), jnp.float32, least / len(split), top_value / len(split)))
        level = level * jnp.repeat(draws, extent[axis_at] // blocks).reshape([-1 if axis == axis_at else 1 for axis in range(len(extent))])
    return level


def normal_values(stream_key, extent, spread, bound, split=(), held_as=jnp.bfloat16):
    gain = shard_levels(stream_key, extent, split, -0.22, 0.18) if split else 1.0
    values = jax.random.normal(stream_key, extent, jnp.float32) * spread * gain
    return jnp.minimum(jnp.maximum(values, -bound), bound).astype(held_as)


def setup_inputs(seed: int = 0) -> dict:
    arg_keys = jax.random.split(jax.random.key(seed), 6)
    field = normal_values(arg_keys[0], (MEMBERS, NZ, C, NX, NY), 1.0, 6.0, ((0, 4), (1, 64)))
    weight = normal_values(arg_keys[1], (KK, K, C * C), (C // 16) ** -0.5, 4.0, ((0, 64),))
    local_weight = normal_values(arg_keys[2], (C, C), C ** -0.5, 1.0)
    bias = normal_values(arg_keys[3], (C,), 0.5, 3.0, (), jnp.float32)
    cotangent = normal_values(arg_keys[4], (MEMBERS, NZ, C, NX, NY), 1.0, 6.0, ((0, 4), (1, 64)))
    return dict(field=field, weight=weight, local_weight=local_weight, bias=bias, cotangent=cotangent)


def basis_table(modes, length):
    frequency = jnp.arange(modes, dtype=jnp.int32) - modes // 2
    points = jnp.arange(length, dtype=jnp.int32)
    product = frequency[:, None] * points[None, :] % length
    angles = product.astype(jnp.float32) * (2.0 * math.pi / length)
    return (jnp.cos(angles) + jnp.sin(angles)) / math.sqrt(length)

def reference(field, weight, local_weight, bias, cotangent):
    highest = lax.Precision.HIGHEST
    basis_y = basis_table(K, NY)
    basis_round = lax.optimization_barrier(basis_y.astype(jnp.bfloat16)).astype(jnp.float32)
    basis_x = basis_table(K, NX)
    basis_z = basis_table(K, NZ)
    mixing = weight.astype(jnp.float32).reshape(K * K, K, C, C)
    local_f32 = local_weight.astype(jnp.float32)
    bias_f32 = bias.astype(jnp.float32)

    def project(data):
        along_y = jnp.einsum('zcxy,ky->zcxk', data.astype(jnp.float32), basis_round, precision=highest)
        along_x = jnp.einsum('zcxk,jx->zcjk', along_y, basis_x, precision=highest).reshape(NZ, C, K * K)
        return jnp.einsum('zcp,kz->kcp', along_x, basis_z, precision=highest)

    def synthesize(coefs):
        along_z = jnp.einsum('kcp,kz->zcp', coefs, basis_z, precision=highest).reshape(NZ, C, K, K)
        along_x = jnp.einsum('zcjk,jx->zcxk', along_z, basis_x, precision=highest)
        return jnp.einsum('zcxk,ky->zcxy', along_x, basis_y, precision=highest)

    def member_step(carry, inputs):
        grad_mixing, grad_local, grad_bias = carry
        values, upstream = inputs
        values_f32 = values.astype(jnp.float32)
        coefs = project(values)
        mixed = jnp.einsum('kcp,pkco->kop', coefs, mixing, precision=highest)
        linear = jnp.einsum('zcxy,co->zoxy', values_f32, local_f32, precision=highest)
        before = synthesize(mixed) + linear + bias_f32[None, :, None, None]
        result, pullback = jax.vjp(jax.nn.gelu, before)
        slope, = pullback(upstream.astype(jnp.float32))
        slope_round = lax.optimization_barrier(slope.astype(jnp.bfloat16))
        slope_f32 = slope_round.astype(jnp.float32)
        grad_local = grad_local + jnp.einsum('zcxy,zoxy->co', values_f32, slope_f32, precision=highest)
        grad_bias = grad_bias + lax.optimization_barrier(jnp.sum(slope_f32, axis=(0, 2, 3)))
        back_coefs = project(slope_round)
        grad_mixing = grad_mixing + jnp.einsum('kcp,kop->pkco', coefs, back_coefs, precision=highest)
        back_modes = jnp.einsum('kop,pkco->kcp', back_coefs, mixing, precision=highest)
        grad_values = synthesize(back_modes) + jnp.einsum('zoxy,co->zcxy', slope_f32, local_f32, precision=highest)
        return ((grad_mixing, grad_local, grad_bias), (result.astype(jnp.bfloat16), grad_values.astype(jnp.bfloat16)))
    start = (jnp.zeros((K * K, K, C, C), jnp.float32), jnp.zeros((C, C), jnp.float32), jnp.zeros((C,), jnp.float32))
    totals, stacked = lax.scan(member_step, start, (field, cotangent))
    grad_mixing, grad_local, grad_bias = totals
    output, grad_field = stacked
    return (output, grad_field, grad_mixing.reshape(K * K, K, C * C), grad_local, grad_bias)
```

```python
import functools
import math

import jax
import jax.numpy as jnp
import ml_dtypes
import numpy as np
from jax import lax
from jax.experimental import pallas as pl
from jax.experimental.pallas import tpu as pltpu
from jax.sharding import PartitionSpec as P

BF = jnp.bfloat16
F32 = jnp.float32
MESH = pl.DeviceIdType.MESH
C = 32
N = 128
K = 32
NZ = 64
XB = 16
ROOT = math.sqrt(2.0 / math.pi)


def basis_table(modes, length):
    frequency = np.arange(modes, dtype=np.int32) - modes // 2
    points = np.arange(length, dtype=np.int32)
    product = frequency[:, None] * points[None, :] % length
    angles = product.astype(np.float32) * np.float32(2.0 * math.pi / length)
    return (np.cos(angles) + np.sin(angles)) / np.float32(math.sqrt(length))


def split_table(table):
    high = table.astype(ml_dtypes.bfloat16)
    low = (table - high.astype(np.float32)).astype(ml_dtypes.bfloat16)
    return high, low


def three(table):
    high, low = split_table(table)
    return np.concatenate([high, high, low], axis=1)


def tables():
    basis = basis_table(K, N)
    slots = np.arange(NZ)
    basis_z = basis_table(K, NZ)[:, slots % 32 * 2 + slots // 32]
    by16 = basis.astype(ml_dtypes.bfloat16).astype(np.float32)
    wide = np.zeros((2, 8, 16, 8, N), np.float32)
    for c in range(8):
        wide[:, c, :, c, :] = by16.reshape(2, 16, N)
    wide = wide.reshape(256, 8 * N)
    eye8, eye32 = np.eye(8, dtype=np.float32), np.eye(32, dtype=np.float32)
    spread = np.repeat(np.repeat(eye8, 16, axis=0), 32, axis=1)
    to_modes = np.tile(np.repeat(eye32, 16, axis=1), (4, 1))
    from_modes = to_modes.T.reshape(4, 128, 128)
    rows = np.repeat(eye32, XB, axis=0)
    lanes = np.zeros((512, 128), np.float32)
    lanes[:, :32] = rows
    return dict(
        wide_t=wide.T.copy(),
        bx=three(basis),
        wide=wide,
        bz=three(basis_z),
        spread=np.concatenate([spread, spread], axis=0),
        to_modes=np.concatenate([to_modes, to_modes], axis=0),
        bzt=three(basis_z.T),
        bxt=three(basis.T),
        rows=rows,
        rows_t=rows.T.copy(),
        lanes=lanes,
        from_modes=np.concatenate([from_modes, from_modes], axis=1),
        gather=np.concatenate([spread.T, spread.T], axis=0),
    )


TABLES = {name: np.asarray(table).astype(ml_dtypes.bfloat16) for name, table in tables().items()}
NAMES = tuple(TABLES)


def split(value):
    high = value.astype(BF)
    return high, (value - high.astype(F32)).astype(BF)


def dot(a, b):
    return jnp.dot(a, b, preferred_element_type=F32)


def dot_nt(a, b):
    return lax.dot_general(a, b, (((1,), (1,)), ((), ())), preferred_element_type=F32)


def dot_three(table, value):
    high, low = split(value)
    return dot(table, jnp.concatenate([high, low, high], axis=0))


def kernel(n_slab, n_ens, field, weight, lw, bias, cot, *rest):
    consts = dict(zip(NAMES, rest[: len(NAMES)]))
    rest = rest[len(NAMES) :]
    out, gf, gs, gl_out, gb_out = rest[:5]
    rest = rest[5:]
    tab = dict(zip(NAMES, rest[: len(NAMES)]))
    rest = rest[len(NAMES) :]
    (
        field_v, cot_v, w_v, pre, out_v, slope_v, gf_v, gs_v, kl_f, kl_b, s2, cexp, gacc, bsum,
        send, recv, call, ball, glsend, glrecv, glall, glfin_send, glfin,
        load_sem, store_sem, tab_sem, send_sem, recv_sem, ens_send, ens_recv, gl_send, gl_recv,
    ) = rest
    me = lax.axis_index("slab")
    mine = lax.axis_index("ens")

    loads = [
        pltpu.make_async_copy(field, field_v, load_sem.at[0]),
        pltpu.make_async_copy(cot, cot_v, load_sem.at[1]),
        pltpu.make_async_copy(weight, w_v, load_sem.at[2]),
    ]
    tab_loads = {
        name: pltpu.make_async_copy(consts[name], tab[name], tab_sem.at[at])
        for at, name in enumerate(NAMES)
    }
    tab_loads["wide_t"].start()
    loads[0].start()
    for name in NAMES[1:]:
        tab_loads[name].start()
    loads[1].start()
    loads[2].start()

    barrier = pltpu.get_barrier_semaphore()

    def greet(at, carry):
        pl.semaphore_signal(barrier, inc=1, device_id={"slab": lax.rem(me + at, n_slab)}, device_id_type=MESH)
        return carry

    lax.fori_loop(1, n_slab, greet, 0)
    for at in range(1, n_ens):
        pl.semaphore_signal(barrier, inc=1, device_id={"ens": lax.rem(mine + at, n_ens)}, device_id_type=MESH)

    def project(data, phase):
        for g in range(4):
            total = None
            for pair in range(4):
                at = g * 8 + pair * 2
                part = dot(
                    jnp.concatenate([data[at], data[at + 1]], axis=1),
                    tab["wide_t"][pair * 256 : (pair + 1) * 256, :],
                )
                total = part if total is None else total + part
            modes = dot_three(tab["bx"][...], total)
            send[phase, :32, g, :] = modes[:, :128]
            send[phase, 32:, g, :] = modes[:, 128:]

    def exchange(phase):
        def one(at, carry):
            peer = lax.rem(me + at, n_slab)
            pltpu.make_async_remote_copy(
                src_ref=send.at[phase, slot(peer)],
                dst_ref=recv.at[phase, slot(me)],
                send_sem=send_sem.at[phase],
                recv_sem=recv_sem.at[phase],
                device_id={"slab": peer},
                device_id_type=MESH,
            ).start()
            return carry

        lax.fori_loop(1, n_slab, one, 0)
        recv[phase, slot(me)] = send[phase, slot(me)]

    def share(source, target, at_sem):
        for at in range(1, n_ens):
            pltpu.make_async_remote_copy(
                src_ref=source,
                dst_ref=target,
                send_sem=ens_send.at[at_sem],
                recv_sem=ens_recv.at[at_sem],
                device_id={"ens": lax.rem(mine + at, n_ens)},
                device_id_type=MESH,
            ).start()

    def wait_share(ref, at_sem):
        some = ref.at[pl.ds(0, n_ens - 1)]
        pltpu.make_async_copy(some, some, ens_recv.at[at_sem]).wait()

    def wait_share_sent(ref, at_sem):
        some = ref.at[pl.ds(0, n_ens - 1)]
        pltpu.make_async_copy(some, some, ens_send.at[at_sem]).wait()

    def spread_out(source, target, at_sem, row):
        def one(at, carry):
            peer = lax.rem(me + at, n_slab)
            pltpu.make_async_remote_copy(
                src_ref=source.at[peer // 2] if row else source.at[0],
                dst_ref=target.at[slot(me)],
                send_sem=gl_send.at[at_sem],
                recv_sem=gl_recv.at[at_sem],
                device_id={"slab": peer},
                device_id_type=MESH,
            ).start()
            return carry

        lax.fori_loop(1, n_slab, one, 0)

    def owned(phase):
        planes = jnp.concatenate([recv[phase, :, g, :] for g in range(4)], axis=1)
        return dot_three(tab["bz"][...], planes)

    def planes_out(phase, modes):
        planes = dot_three(tab["bzt"][...], modes)
        for g in range(4):
            send[phase, :, g, :] = planes[:, g * 128 : (g + 1) * 128]

    def own_pair(chunk, lanes):
        row = lax.broadcasted_iota(jnp.int32, (128, lanes), 0) // 32 + chunk * 4
        lane = lax.rem(lax.broadcasted_iota(jnp.int32, (128, lanes), 1), 16)
        return row == lane

    def masked(modes, keep):
        tall = jnp.concatenate([modes] * 4, axis=0)
        high, low = split(jnp.where(keep, tall, 0.0))
        return jnp.concatenate([high, low], axis=1)

    def fold(value, keep):
        value = jnp.where(keep, value, 0.0)
        return value[0:32] + value[32:64] + value[64:96] + value[96:128]

    def to_channels(modes, keep):
        total = None
        for g in range(4):
            part = dot(masked(modes[:, g * 128 : (g + 1) * 128], keep), tab["from_modes"][g])
            total = part if total is None else total + part
        return total

    def weights_of(chunk, g):
        return w_v[pl.ds(chunk * 4, 4), :, g * 256 : (g + 1) * 256].reshape(128, 256).astype(F32)

    def narrow(phase):
        for g in range(4):
            modes = jnp.concatenate([recv[phase, :32, g, :], recv[phase, 32:, g, :]], axis=1)
            s2[g] = dot_three(tab["bxt"][...], modes).astype(BF)

    def block_of(ref, at):
        a = ref[:, pl.ds(pl.multiple_of(at * 2 * XB, 2 * XB), XB), :].reshape(C * XB, N)
        b = ref[:, pl.ds(pl.multiple_of(at * 2 * XB + XB, XB), XB), :].reshape(C * XB, N)
        return jnp.concatenate([a, b], axis=1)

    def pointwise(matrix, data):
        def step(at, carry):
            value = dot(matrix[...], block_of(data, at))
            pre[:, pl.ds(pl.multiple_of(at * 2 * XB, 2 * XB), XB), :] = value[:, :N].reshape(C, XB, N)
            pre[:, pl.ds(pl.multiple_of(at * 2 * XB + XB, XB), XB), :] = value[:, N:].reshape(C, XB, N)
            return carry

        lax.fori_loop(0, N // (2 * XB), step, 0)

    tab_loads["wide_t"].wait()
    tab_loads["bx"].wait()
    loads[0].wait()
    project(field_v, 0)
    pl.semaphore_wait(barrier, n_slab - 1 + n_ens - 1)
    exchange(0)

    for name in NAMES[2:]:
        tab_loads[name].wait()
    loads[1].wait()
    loads[2].wait()
    tall = dot(dot_nt(tab["rows"][...], lw[...]).astype(BF), tab["rows_t"][...])
    same = lax.rem(lax.broadcasted_iota(jnp.int32, (512, 512), 0), XB) == lax.rem(
        lax.broadcasted_iota(jnp.int32, (512, 512), 1), XB
    )
    kl_f[...] = jnp.where(same, tall, 0.0).astype(BF)
    tall = dot(dot(tab["rows"][...], lw[...]).astype(BF), tab["rows_t"][...])
    kl_b[...] = jnp.where(same, tall, 0.0).astype(BF)
    pointwise(kl_f, field_v)

    wait_all(recv, recv_sem, 0)
    coefs = owned(0)
    call[mine] = coefs
    share(call.at[mine], call.at[mine], 0)

    def mix(chunk, total):
        keep = own_pair(chunk, 128)
        part = None
        for g in range(4):
            wide = dot(masked(coefs_at(call, mine, g), keep), tab["spread"][...])
            value = wide * weights_of(chunk, g)
            value = value[:, :128] + value[:, 128:]
            part = value if part is None else part + value
        high, low = split(part)
        value = dot(jnp.concatenate([high, low], axis=1), tab["to_modes"][...])
        return total + fold(value, own_pair(chunk, 512))

    mixed = lax.fori_loop(0, 4, mix, jnp.zeros((K, 512), F32))
    planes_out(1, mixed)
    exchange(1)

    wait_share(call, 0)

    def spread_member(step, carry):
        member, chunk = step // 4, lax.rem(step, 4)
        keep = own_pair(chunk, 128)
        for g in range(4):
            cexp[member, pl.ds(pl.multiple_of(chunk * 128, 128), 128), g * 256 : (g + 1) * 256] = dot(
                masked(coefs_at(call, member, g), keep), tab["spread"][...]
            )
        return carry

    lax.fori_loop(0, 4 * n_ens, spread_member, 0)

    wait_all(recv, recv_sem, 1)
    narrow(1)
    bsum[...] = jnp.zeros_like(bsum)

    def activate(step, carry):
        group, pair = step // 4, lax.rem(step, 4)
        both = dot(s2[group], tab["wide"][:, pl.ds(pl.multiple_of(pair * 256, 256), 256)])
        for half in range(2):
            o = step * 2 + half
            v = both[:, half * 128 : (half + 1) * 128] + pre[o] + bias[o]
            square = v * v
            t = jnp.tanh(ROOT * (v + 0.044715 * (v * square)))
            out_v[o] = (0.5 * v * (1.0 + t)).astype(BF)
            grad = 0.5 * (1.0 + t) + (0.5 * ROOT) * v * (1.0 - t * t) * (1.0 + (3 * 0.044715) * square)
            slope = (cot_v[o].astype(F32) * grad).astype(BF)
            slope_v[o] = slope
            bsum[pl.ds(32 + o, 1), :] = jnp.sum(slope.astype(F32), axis=0, keepdims=True)
        return carry

    lax.fori_loop(0, C // 2, activate, 0)
    stores = [pltpu.make_async_copy(out_v, out, store_sem.at[0])]
    stores[0].start()

    project(slope_v, 2)
    exchange(2)

    gacc[...] = jnp.zeros_like(gacc)

    def outer(at, carry):
        gacc[...] += dot_nt(block_of(field_v, at), block_of(slope_v, at))
        return carry

    lax.fori_loop(0, N // (2 * XB), outer, 0)
    same = lax.rem(lax.broadcasted_iota(jnp.int32, (512, 512), 0), XB) == lax.rem(
        lax.broadcasted_iota(jnp.int32, (512, 512), 1), XB
    )
    rows = jnp.sum(jnp.where(same, gacc[...], 0.0).reshape(C, XB, 512), axis=1)
    high, low = split(rows)
    grad_rows = dot(high, tab["lanes"][...]) + dot(low, tab["lanes"][...])
    high, low = split(bsum[...])
    ones = jnp.ones((8, 128), BF)
    bias_row = (dot_nt(ones, high) + dot_nt(ones, low))[0:1]
    glsend[:, 0, :] = grad_rows + bias_row
    spread_out(glsend, glrecv, 0, True)
    glrecv[slot(me)] = glsend[me // 2]
    pointwise(kl_b, slope_v)

    wait_all(recv, recv_sem, 2)
    back = owned(2)
    ball[mine] = back
    share(ball.at[mine], ball.at[mine], 1)

    def mix_back(chunk, total):
        keep = own_pair(chunk, 128)
        four = to_channels(ball[mine], keep)
        four = jnp.concatenate([four, four], axis=1)
        parts = []
        for g in range(4):
            high, low = split(weights_of(chunk, g) * four)
            value = dot(jnp.concatenate([high, low], axis=1), tab["gather"][...])
            parts.append(fold(value, keep))
        return total + jnp.concatenate(parts, axis=1)

    back_modes = lax.fori_loop(0, 4, mix_back, jnp.zeros((K, 512), F32))
    planes_out(3, back_modes)
    exchange(3)

    wait_block(glrecv, gl_recv, 0)
    glall[mine] = jnp.sum(glrecv[...], axis=0)
    share(glall.at[mine], glall.at[mine], 2)
    wait_share(ball, 1)
    wait_share(glall, 2)
    glfin_send[0] = glall[0] + glall[1] + glall[2] + glall[3]
    spread_out(glfin_send, glfin, 1, False)
    glfin[slot(me)] = glfin_send[0]

    def spectral(chunk, carry):
        keep = own_pair(chunk, 128)
        rows = pl.ds(pl.multiple_of(chunk * 128, 128), 128)
        fours = []
        for member in range(n_ens):
            four = to_channels(ball[member], keep)
            fours.append(jnp.concatenate([four, four], axis=1))
        for g in range(4):
            total = None
            for member in range(n_ens):
                part = cexp[member, rows, g * 256 : (g + 1) * 256] * fours[member]
                total = part if total is None else total + part
            gs_v[pl.ds(chunk * 4, 4), :, g * 256 : (g + 1) * 256] = total.reshape(4, 32, 256)
        return carry

    lax.fori_loop(0, 4, spectral, 0)
    stores.append(pltpu.make_async_copy(gs_v, gs, store_sem.at[1]))
    stores[1].start()

    wait_all(recv, recv_sem, 3)
    narrow(3)

    def finish(step, carry):
        group, pair = step // 4, lax.rem(step, 4)
        both = dot(s2[group], tab["wide"][:, pl.ds(pl.multiple_of(pair * 256, 256), 256)])
        for half in range(2):
            o = step * 2 + half
            gf_v[o] = (both[:, half * 128 : (half + 1) * 128] + pre[o]).astype(BF)
        return carry

    lax.fori_loop(0, C // 2, finish, 0)
    stores.append(pltpu.make_async_copy(gf_v, gf, store_sem.at[2]))
    stores[2].start()

    wait_block(glfin, gl_recv, 1)
    final = glfin[:32, 0, :]
    gl_out[...] = final[:, :32]
    gb_out[...] = final[0:1, 32:64]

    for phase in range(4):
        wait_all(send, send_sem, phase)
    wait_block(glrecv, gl_send, 0)
    wait_block(glfin, gl_send, 1)
    wait_share_sent(call, 0)
    wait_share_sent(ball, 1)
    wait_share_sent(glall, 2)
    for store in stores:
        store.wait()


def slot(device):
    return lax.rem(device, 2) * 32 + device // 2


def coefs_at(ref, member, g):
    return ref[member, :, g * 128 : (g + 1) * 128]


def wait_all(ref, sem, phase):
    some = ref.at[phase, pl.ds(0, NZ - 1)]
    pltpu.make_async_copy(some, some, sem.at[phase]).wait()


def wait_block(ref, sem, at):
    some = ref.at[pl.ds(0, NZ - 1)]
    pltpu.make_async_copy(some, some, sem.at[at]).wait()


def local(n_slab, n_ens, field, weight, local_weight, bias, cotangent):
    consts = [jnp.asarray(TABLES[name]) for name in NAMES]
    any_spec = pl.BlockSpec(memory_space=pl.ANY)
    vmem = pl.BlockSpec(memory_space=pltpu.VMEM)
    smem = pl.BlockSpec(memory_space=pltpu.SMEM)
    image = (C, N, N)
    dma = pltpu.SemaphoreType.DMA
    outs = pl.pallas_call(
        functools.partial(kernel, n_slab, n_ens),
        out_shape=(
            jax.ShapeDtypeStruct(image, BF),
            jax.ShapeDtypeStruct(image, BF),
            jax.ShapeDtypeStruct((16, 32, 1024), F32),
            jax.ShapeDtypeStruct((32, 32), F32),
            jax.ShapeDtypeStruct((1, 32), F32),
        ),
        in_specs=[any_spec, any_spec, vmem, smem, any_spec] + [any_spec] * len(NAMES),
        out_specs=(any_spec, any_spec, any_spec, vmem, vmem),
        scratch_shapes=[pltpu.VMEM(TABLES[name].shape, BF) for name in NAMES]
        + [
            pltpu.VMEM(image, BF),
            pltpu.VMEM(image, BF),
            pltpu.VMEM((16, 32, 1024), BF),
            pltpu.VMEM(image, F32),
            pltpu.VMEM(image, BF),
            pltpu.VMEM(image, BF),
            pltpu.VMEM(image, BF),
            pltpu.VMEM((16, 32, 1024), F32),
            pltpu.VMEM((512, 512), BF),
            pltpu.VMEM((512, 512), BF),
            pltpu.VMEM((4, 128, 256), BF),
            pltpu.VMEM((n_ens, 512, 1024), F32),
            pltpu.VMEM((512, 512), F32),
            pltpu.VMEM((128, 128), F32),
            pltpu.VMEM((4, NZ, 4, 128), F32),
            pltpu.VMEM((4, NZ, 4, 128), F32),
            pltpu.VMEM((n_ens, K, 512), F32),
            pltpu.VMEM((n_ens, K, 512), F32),
            pltpu.VMEM((32, 1, 128), F32),
            pltpu.VMEM((NZ, 1, 128), F32),
            pltpu.VMEM((n_ens, 1, 128), F32),
            pltpu.VMEM((1, 1, 128), F32),
            pltpu.VMEM((NZ, 1, 128), F32),
            dma((3,)),
            dma((3,)),
            dma((len(NAMES),)),
            dma((4,)),
            dma((4,)),
            dma((3,)),
            dma((3,)),
            dma((2,)),
            dma((2,)),
        ],
        compiler_params=pltpu.CompilerParams(
            collective_id=0, has_side_effects=True, vmem_limit_bytes=56 * 1024 * 1024
        ),
    )(
        field.reshape(image),
        weight,
        local_weight,
        bias,
        cotangent.reshape(image),
        *consts,
    )
    output, grad_field, grad_spectral, grad_local, grad_bias = outs
    whole = (1, 1) + image
    return (
        output.reshape(whole),
        grad_field.reshape(whole),
        grad_spectral,
        grad_local,
        grad_bias.reshape(32),
    )


def solution(mesh):
    placed = (
        P("ens", "slab", None, None, None),
        P("slab", None, None),
        P(),
        P(),
        P("ens", "slab", None, None, None),
    )
    return jax.shard_map(
        functools.partial(local, mesh.shape["slab"], mesh.shape["ens"]),
        mesh=mesh,
        in_specs=placed,
        out_specs=(
            P("ens", "slab", None, None, None),
            P("ens", "slab", None, None, None),
            P("slab", None, None),
            P(),
            P(),
        ),
        check_vma=False,
    )
```

```python
import functools
import math

import jax
import jax.numpy as jnp
import ml_dtypes
import numpy as np
from jax import lax
from jax.experimental import pallas as pl
from jax.experimental.pallas import tpu as pltpu
from jax.sharding import PartitionSpec as P

BF = jnp.bfloat16
F32 = jnp.float32
MESH = pl.DeviceIdType.MESH
C = 32
N = 128
K = 32
NZ = 64
XB = 16
ROOT = math.sqrt(2.0 / math.pi)


def basis_table(modes, length):
    frequency = np.arange(modes, dtype=np.int32) - modes // 2
    points = np.arange(length, dtype=np.int32)
    product = frequency[:, None] * points[None, :] % length
    angles = product.astype(np.float32) * np.float32(2.0 * math.pi / length)
    return (np.cos(angles) + np.sin(angles)) / np.float32(math.sqrt(length))


def split_table(table):
    high = table.astype(ml_dtypes.bfloat16)
    low = (table - high.astype(np.float32)).astype(ml_dtypes.bfloat16)
    return high, low


def three(table):
    high, low = split_table(table)
    return np.concatenate([high, high, low], axis=1)


def tables():
    basis = basis_table(K, N)
    slots = np.arange(NZ)
    basis_z = basis_table(K, NZ)[:, slots % 32 * 2 + slots // 32]
    by16 = basis.astype(ml_dtypes.bfloat16).astype(np.float32)
    wide = np.zeros((2, 8, 16, 8, N), np.float32)
    for c in range(8):
        wide[:, c, :, c, :] = by16.reshape(2, 16, N)
    wide = wide.reshape(256, 8 * N)
    eye8, eye32 = np.eye(8, dtype=np.float32), np.eye(32, dtype=np.float32)
    spread = np.repeat(np.repeat(eye8, 16, axis=0), 32, axis=1)
    to_modes = np.tile(np.repeat(eye32, 16, axis=1), (4, 1))
    from_modes = to_modes.T.reshape(4, 128, 128)
    rows = np.repeat(eye32, XB, axis=0)
    lanes = np.tile(rows, (1, 4))
    return dict(
        wide_t=wide.T.copy(),
        bx=three(basis),
        wide=wide,
        bz=three(basis_z),
        spread=np.concatenate([spread, spread], axis=0),
        to_modes=np.concatenate([to_modes, to_modes], axis=0),
        bzt=three(basis_z.T),
        bxt=three(basis.T),
        rows=rows,
        rows_t=rows.T.copy(),
        lanes=lanes,
        from_modes=np.concatenate([from_modes, from_modes], axis=1),
        gather=np.concatenate([spread.T, spread.T], axis=0),
    )


TABLES = {name: np.asarray(table).astype(ml_dtypes.bfloat16) for name, table in tables().items()}
NAMES = tuple(TABLES)


def split(value):
    high = value.astype(BF)
    return high, (value - high.astype(F32)).astype(BF)


def dot(a, b):
    return jnp.dot(a, b, preferred_element_type=F32)


def dot_nt(a, b):
    return lax.dot_general(a, b, (((1,), (1,)), ((), ())), preferred_element_type=F32)


def dot_three(table, value):
    high, low = split(value)
    return dot(table, jnp.concatenate([high, low, high], axis=0))


def middle_out(at, size):
    return size // 2 + (at + 1) // 2 * (2 * lax.rem(at + 1, 2) - 1)


def far_first(me, at):
    x = lax.rem(me // 16 + middle_out(lax.rem(at // 2, 4), 4), 4)
    z = lax.rem(lax.rem(me // 2, 8) + middle_out(at // 8, 8), 8)
    return x * 16 + z * 2 + lax.rem(me + 1 + at, 2)


def kernel(n_slab, n_ens, field, weight, lw, bias, cot, *rest):
    consts = dict(zip(NAMES, rest[: len(NAMES)]))
    rest = rest[len(NAMES) :]
    out, gf, gs, gl_out, gb_out = rest[:5]
    rest = rest[5:]
    tab = dict(zip(NAMES, rest[: len(NAMES)]))
    rest = rest[len(NAMES) :]
    (
        field_v, cot_v, w_v, pre, out_v, slope_v, gf_v, gs_v, kl_f, kl_b, cexp, gacc,
        send, recv, call, ball, sums,
        load_sem, store_sem, tab_sem, send_sem, recv_sem, ens_send, ens_recv, sum_send, sum_recv,
    ) = rest
    me = lax.axis_index("slab")
    mine = lax.axis_index("ens")
    x, z, core = me // 16, lax.rem(me // 2, 8), lax.rem(me, 2)

    barrier = pltpu.get_barrier_semaphore()

    def greet(at, carry):
        pl.semaphore_signal(barrier, inc=1, device_id={"slab": lax.rem(me + at, n_slab)}, device_id_type=MESH)
        return carry

    lax.fori_loop(1, n_slab, greet, 0)
    for at in range(1, n_ens):
        pl.semaphore_signal(barrier, inc=1, device_id={"ens": lax.rem(mine + at, n_ens)}, device_id_type=MESH)

    loads = [
        pltpu.make_async_copy(field, field_v, load_sem.at[0]),
        pltpu.make_async_copy(cot, cot_v, load_sem.at[1]),
        pltpu.make_async_copy(weight, w_v, load_sem.at[2]),
    ]
    tab_loads = {
        name: pltpu.make_async_copy(consts[name], tab[name], tab_sem.at[at])
        for at, name in enumerate(NAMES)
    }
    tab_loads["wide_t"].start()
    loads[0].start()
    for name in NAMES[1:]:
        tab_loads[name].start()
    loads[1].start()
    loads[2].start()

    def project(data, pair):
        return dot(jnp.concatenate(data, axis=1), tab["wide_t"][pair * 256 : (pair + 1) * 256, :])

    def exchange(phase):
        def one(at, carry):
            peer = far_first(me, at)
            pltpu.make_async_remote_copy(
                src_ref=send.at[phase, slot(peer)],
                dst_ref=recv.at[phase, slot(me)],
                send_sem=send_sem.at[phase],
                recv_sem=recv_sem.at[phase],
                device_id={"slab": peer},
                device_id_type=MESH,
            ).start()
            return carry

        lax.fori_loop(0, n_slab - 1, one, 0)
        recv[phase, slot(me)] = send[phase, slot(me)]

    def share(source, target, at_sem):
        for at in range(1, n_ens):
            pltpu.make_async_remote_copy(
                src_ref=source,
                dst_ref=target,
                send_sem=ens_send.at[at_sem],
                recv_sem=ens_recv.at[at_sem],
                device_id={"ens": lax.rem(mine + at, n_ens)},
                device_id_type=MESH,
            ).start()

    def wait_share(ref, at_sem):
        some = ref.at[pl.ds(0, n_ens - 1)]
        pltpu.make_async_copy(some, some, ens_recv.at[at_sem]).wait()

    def wait_share_sent(ref, at_sem):
        some = ref.at[pl.ds(0, n_ens - 1)]
        pltpu.make_async_copy(some, some, ens_send.at[at_sem]).wait()

    def share_sums(stage, place, peers):
        for peer in peers:
            pltpu.make_async_remote_copy(
                src_ref=sums.at[stage, place],
                dst_ref=sums.at[stage, place],
                send_sem=sum_send.at[stage],
                recv_sem=sum_recv.at[stage],
                device_id=peer,
                device_id_type=MESH,
            ).start()

    def wait_sums(stage, size, sem):
        some = sums.at[stage, pl.ds(0, size - 1)]
        pltpu.make_async_copy(some, some, sem.at[stage]).wait()

    def owned(phase):
        planes = jnp.concatenate([recv[phase, :, g, :] for g in range(4)], axis=1)
        return dot_three(tab["bz"][...], planes)

    def planes_out(phase, modes):
        planes = dot_three(tab["bzt"][...], modes)
        for g in range(4):
            send[phase, :, g, :] = planes[:, g * 128 : (g + 1) * 128]

    def own_pair(chunk, lanes):
        row = lax.broadcasted_iota(jnp.int32, (128, lanes), 0) // 32 + chunk * 4
        lane = lax.rem(lax.broadcasted_iota(jnp.int32, (128, lanes), 1), 16)
        return row == lane

    def masked(modes, keep):
        tall = jnp.concatenate([modes] * 4, axis=0)
        high, low = split(jnp.where(keep, tall, 0.0))
        return jnp.concatenate([high, low], axis=1)

    def fold(value, keep):
        value = jnp.where(keep, value, 0.0)
        return value[0:32] + value[32:64] + value[64:96] + value[96:128]

    def to_channels(modes, keep):
        total = None
        for g in range(4):
            part = dot(masked(modes[:, g * 128 : (g + 1) * 128], keep), tab["from_modes"][g])
            total = part if total is None else total + part
        return total

    def weights_of(chunk, g):
        return w_v[pl.ds(chunk * 4, 4), :, g * 256 : (g + 1) * 256].reshape(128, 256).astype(F32)

    def narrow(phase, g):
        modes = jnp.concatenate([recv[phase, :32, g, :], recv[phase, 32:, g, :]], axis=1)
        return dot_three(tab["bxt"][...], modes).astype(BF)

    def put(phase, g, total):
        modes = dot_three(tab["bx"][...], total)
        send[phase, :32, g, :] = modes[:, :128]
        send[phase, 32:, g, :] = modes[:, 128:]

    def block_of(ref, at):
        a = ref[:, pl.ds(pl.multiple_of(at * 2 * XB, 2 * XB), XB), :].reshape(C * XB, N)
        b = ref[:, pl.ds(pl.multiple_of(at * 2 * XB + XB, XB), XB), :].reshape(C * XB, N)
        return jnp.concatenate([a, b], axis=1)

    def pointwise(matrix, data):
        def step(at, carry):
            value = dot(matrix[...], block_of(data, at))
            pre[:, pl.ds(pl.multiple_of(at * 2 * XB, 2 * XB), XB), :] = value[:, :N].reshape(C, XB, N)
            pre[:, pl.ds(pl.multiple_of(at * 2 * XB + XB, XB), XB), :] = value[:, N:].reshape(C, XB, N)
            return carry

        lax.fori_loop(0, N // (2 * XB), step, 0)

    tab_loads["wide_t"].wait()
    tab_loads["bx"].wait()
    loads[0].wait()
    for g in range(4):
        total = None
        for pair in range(4):
            at = g * 8 + pair * 2
            part = project([field_v[at], field_v[at + 1]], pair)
            total = part if total is None else total + part
        put(0, g, total)
    pl.semaphore_wait(barrier, n_slab - 1 + n_ens - 1)
    exchange(0)

    for name in NAMES[2:]:
        tab_loads[name].wait()
    loads[1].wait()
    loads[2].wait()
    tall = dot(dot_nt(tab["rows"][...], lw[...]).astype(BF), tab["rows_t"][...])
    same = lax.rem(lax.broadcasted_iota(jnp.int32, (512, 512), 0), XB) == lax.rem(
        lax.broadcasted_iota(jnp.int32, (512, 512), 1), XB
    )
    kl_f[...] = jnp.where(same, tall, 0.0).astype(BF)
    tall = dot(dot(tab["rows"][...], lw[...]).astype(BF), tab["rows_t"][...])
    kl_b[...] = jnp.where(same, tall, 0.0).astype(BF)
    pointwise(kl_f, field_v)

    wait_all(recv, recv_sem, 0)
    coefs = owned(0)
    call[mine] = coefs

    def mix(chunk, total):
        keep = own_pair(chunk, 128)
        part = None
        for g in range(4):
            wide = dot(masked(coefs_at(call, mine, g), keep), tab["spread"][...])
            value = wide * weights_of(chunk, g)
            value = value[:, :128] + value[:, 128:]
            part = value if part is None else part + value
        high, low = split(part)
        value = dot(jnp.concatenate([high, low], axis=1), tab["to_modes"][...])
        return total + fold(value, own_pair(chunk, 512))

    mixed = lax.fori_loop(0, 4, mix, jnp.zeros((K, 512), F32), unroll=True)
    planes_out(1, mixed)
    exchange(1)


    def spread_member(at, carry):
        member = lax.rem(mine + at, n_ens)
        for chunk in range(4):
            keep = own_pair(chunk, 128)
            for g in range(4):
                cexp[member, chunk * 128 : (chunk + 1) * 128, g * 256 : (g + 1) * 256] = dot(
                    masked(coefs_at(call, member, g), keep), tab["spread"][...]
                )
        return carry

    spread_member(0, 0)

    wait_all(recv, recv_sem, 1)
    share(call.at[mine], call.at[mine], 0)
    for g in range(4):
        narrowed = narrow(1, g)
        total = None
        for pair in range(4):
            both = dot(narrowed, tab["wide"][:, pair * 256 : (pair + 1) * 256])
            slopes = []
            for half in range(2):
                o = g * 8 + pair * 2 + half
                v = both[:, half * 128 : (half + 1) * 128] + (pre[o] + bias[o])
                cubic = (ROOT * 0.044715) * (v * v)
                t = jnp.tanh(v * (ROOT + cubic))
                h = 0.5 * v
                out_v[o] = (h + h * t).astype(BF)
                grad = (0.5 + 0.5 * t) + (h * (1.0 - t * t)) * (ROOT + 3.0 * cubic)
                slopes.append((cot_v[o].astype(F32) * grad).astype(BF))
                slope_v[o] = slopes[-1]
            part = project(slopes, pair)
            total = part if total is None else total + part
        put(2, g, total)
    exchange(2)
    stores = [pltpu.make_async_copy(out_v, out, store_sem.at[0])]
    stores[0].start()

    gacc[...] = jnp.zeros_like(gacc)

    def outer(at, carry):
        ones = jnp.ones((XB, 2 * N), BF)
        gacc[...] += dot_nt(jnp.concatenate([block_of(field_v, at), ones], axis=0), block_of(slope_v, at))
        return carry

    lax.fori_loop(0, N // (2 * XB), outer, 0)
    same = lax.rem(lax.broadcasted_iota(jnp.int32, (512, 512), 0), XB) == lax.rem(
        lax.broadcasted_iota(jnp.int32, (512, 512), 1), XB
    )
    rows = jnp.sum(jnp.where(same, gacc[: C * XB], 0.0).reshape(C, XB, 512), axis=1)
    bias_rows = gacc[C * XB : C * XB + XB]
    high, low = split(jnp.concatenate([rows, bias_rows], axis=0))
    rows = dot(high, tab["lanes"][...]) + dot(low, tab["lanes"][...])
    lane = lax.broadcasted_iota(jnp.int32, (8, 128), 1) // 32
    packed = jnp.zeros((8, 128), F32)
    for part in range(4):
        packed = packed + jnp.where(lane == part, rows[part * 8 : (part + 1) * 8], 0.0)
    near = x * 2 + core
    sums[0, near, :8] = packed
    sums[0, near, 8:] = rows[C : C + 8]
    peers = [lax.rem(near + at, 8) for at in range(1, 8)]
    share_sums(0, near, [{"slab": peer // 2 * 16 + z * 2 + lax.rem(peer, 2)} for peer in peers])
    pointwise(kl_b, slope_v)
    wait_share(call, 0)
    lax.fori_loop(1, n_ens, spread_member, 0)
    wait_sums(0, 8, sum_recv)
    sums[1, z] = jnp.sum(sums[0], axis=0)
    share_sums(1, z, [{"slab": x * 16 + lax.rem(z + at, 8) * 2 + core} for at in range(1, 8)])

    wait_all(recv, recv_sem, 2)
    back = owned(2)
    ball[mine] = back
    share(ball.at[mine], ball.at[mine], 1)

    def mix_back(chunk, total):
        keep = own_pair(chunk, 128)
        four = to_channels(ball[mine], keep)
        four = jnp.concatenate([four, four], axis=1)
        parts = []
        for g in range(4):
            high, low = split(weights_of(chunk, g) * four)
            value = dot(jnp.concatenate([high, low], axis=1), tab["gather"][...])
            parts.append(fold(value, keep))
        return total + jnp.concatenate(parts, axis=1)

    back_modes = lax.fori_loop(0, 4, mix_back, jnp.zeros((K, 512), F32), unroll=True)
    planes_out(3, back_modes)
    exchange(3)


    wait_sums(1, 8, sum_recv)
    sums[2, mine] = jnp.sum(sums[1], axis=0)
    share_sums(2, mine, [{"ens": lax.rem(mine + at, n_ens)} for at in range(1, n_ens)])
    wait_share(ball, 1)

    def spectral(chunk, carry):
        keep = own_pair(chunk, 128)
        rows = pl.ds(pl.multiple_of(chunk * 128, 128), 128)
        fours = []
        for member in range(n_ens):
            four = to_channels(ball[member], keep)
            fours.append(jnp.concatenate([four, four], axis=1))
        for g in range(4):
            total = None
            for member in range(n_ens):
                part = cexp[member, rows, g * 256 : (g + 1) * 256] * fours[member]
                total = part if total is None else total + part
            gs_v[pl.ds(chunk * 4, 4), :, g * 256 : (g + 1) * 256] = total.reshape(4, 32, 256)
        return carry

    lax.fori_loop(0, 4, spectral, 0)
    stores.append(pltpu.make_async_copy(gs_v, gs, store_sem.at[1]))
    stores[1].start()

    wait_all(recv, recv_sem, 3)
    for g in range(4):
        narrowed = narrow(3, g)
        for pair in range(4):
            both = dot(narrowed, tab["wide"][:, pair * 256 : (pair + 1) * 256])
            for half in range(2):
                o = g * 8 + pair * 2 + half
                gf_v[o] = (both[:, half * 128 : (half + 1) * 128] + pre[o]).astype(BF)
    stores.append(pltpu.make_async_copy(gf_v, gf, store_sem.at[2]))
    stores[2].start()

    wait_sums(2, n_ens, sum_recv)
    total = sums[2, 0] + sums[2, 1] + sums[2, 2] + sums[2, 3]
    for part in range(4):
        gl_out[part * 8 : (part + 1) * 8, :] = total[:8, part * 32 : (part + 1) * 32]
    gb_out[...] = total[8:9, :32]

    for phase in range(4):
        wait_all(send, send_sem, phase)
    for stage, size in enumerate((8, 8, n_ens)):
        wait_sums(stage, size, sum_send)
    wait_share_sent(call, 0)
    wait_share_sent(ball, 1)
    for store in stores:
        store.wait()


def slot(device):
    return lax.rem(device, 2) * 32 + device // 2


def coefs_at(ref, member, g):
    return ref[member, :, g * 128 : (g + 1) * 128]


def wait_all(ref, sem, phase):
    some = ref.at[phase, pl.ds(0, NZ - 1)]
    pltpu.make_async_copy(some, some, sem.at[phase]).wait()


def local(n_slab, n_ens, field, weight, local_weight, bias, cotangent):
    consts = [jnp.asarray(TABLES[name]) for name in NAMES]
    any_spec = pl.BlockSpec(memory_space=pl.ANY)
    vmem = pl.BlockSpec(memory_space=pltpu.VMEM)
    smem = pl.BlockSpec(memory_space=pltpu.SMEM)
    image = (C, N, N)
    dma = pltpu.SemaphoreType.DMA
    outs = pl.pallas_call(
        functools.partial(kernel, n_slab, n_ens),
        out_shape=(
            jax.ShapeDtypeStruct(image, BF),
            jax.ShapeDtypeStruct(image, BF),
            jax.ShapeDtypeStruct((16, 32, 1024), F32),
            jax.ShapeDtypeStruct((32, 32), F32),
            jax.ShapeDtypeStruct((1, 32), F32),
        ),
        in_specs=[any_spec, any_spec, vmem, smem, any_spec] + [any_spec] * len(NAMES),
        out_specs=(any_spec, any_spec, any_spec, vmem, vmem),
        scratch_shapes=[pltpu.VMEM(TABLES[name].shape, BF) for name in NAMES]
        + [
            pltpu.VMEM(image, BF),
            pltpu.VMEM(image, BF),
            pltpu.VMEM((16, 32, 1024), BF),
            pltpu.VMEM(image, F32),
            pltpu.VMEM(image, BF),
            pltpu.VMEM(image, BF),
            pltpu.VMEM(image, BF),
            pltpu.VMEM((16, 32, 1024), F32),
            pltpu.VMEM((512, 512), BF),
            pltpu.VMEM((512, 512), BF),
            pltpu.VMEM((n_ens, 512, 1024), F32),
            pltpu.VMEM((512 + XB, 512), F32),
            pltpu.VMEM((4, NZ, 4, 128), F32),
            pltpu.VMEM((4, NZ, 4, 128), F32),
            pltpu.VMEM((n_ens, K, 512), F32),
            pltpu.VMEM((n_ens, K, 512), F32),
            pltpu.VMEM((3, 8, 16, 128), F32),
            dma((3,)),
            dma((3,)),
            dma((len(NAMES),)),
            dma((4,)),
            dma((4,)),
            dma((2,)),
            dma((2,)),
            dma((3,)),
            dma((3,)),
        ],
        compiler_params=pltpu.CompilerParams(
            collective_id=0, has_side_effects=True, vmem_limit_bytes=56 * 1024 * 1024
        ),
    )(
        field.reshape(image),
        weight,
        local_weight,
        bias,
        cotangent.reshape(image),
        *consts,
    )
    output, grad_field, grad_spectral, grad_local, grad_bias = outs
    whole = (1, 1) + image
    return (
        output.reshape(whole),
        grad_field.reshape(whole),
        grad_spectral,
        grad_local,
        grad_bias.reshape(32),
    )


def solution(mesh):
    placed = (
        P("ens", "slab", None, None, None),
        P("slab", None, None),
        P(),
        P(),
        P("ens", "slab", None, None, None),
    )
    return jax.shard_map(
        functools.partial(local, mesh.shape["slab"], mesh.shape["ens"]),
        mesh=mesh,
        in_specs=placed,
        out_specs=(
            P("ens", "slab", None, None, None),
            P("ens", "slab", None, None, None),
            P("slab", None, None),
            P(),
            P(),
        ),
        check_vma=False,
    )
```

```python
import functools
import math

import jax
import jax.numpy as jnp
import ml_dtypes
import numpy as np
from jax import lax
from jax.experimental import pallas as pl
from jax.experimental.pallas import tpu as pltpu
from jax.sharding import PartitionSpec as P

BF = jnp.bfloat16
F32 = jnp.float32
MESH = pl.DeviceIdType.MESH
C = 32
N = 128
K = 32
NZ = 64
XB = 16
ROOT = math.sqrt(2.0 / math.pi)


def basis_table(modes, length):
    frequency = np.arange(modes, dtype=np.int32) - modes // 2
    points = np.arange(length, dtype=np.int32)
    product = frequency[:, None] * points[None, :] % length
    angles = product.astype(np.float32) * np.float32(2.0 * math.pi / length)
    return (np.cos(angles) + np.sin(angles)) / np.float32(math.sqrt(length))


def split_table(table):
    high = table.astype(ml_dtypes.bfloat16)
    low = (table - high.astype(np.float32)).astype(ml_dtypes.bfloat16)
    return high, low


def three(table):
    high, low = split_table(table)
    return np.concatenate([high, high, low], axis=1)


def tables():
    basis = basis_table(K, N)
    slots = np.arange(NZ)
    basis_z = basis_table(K, NZ)[:, slots % 32 * 2 + slots // 32]
    by16 = basis.astype(ml_dtypes.bfloat16).astype(np.float32)
    wide = np.zeros((2, 8, 16, 8, N), np.float32)
    for c in range(8):
        wide[:, c, :, c, :] = by16.reshape(2, 16, N)
    wide = wide.reshape(256, 8 * N)
    eye8, eye32 = np.eye(8, dtype=np.float32), np.eye(32, dtype=np.float32)
    spread = np.repeat(np.repeat(eye8, 16, axis=0), 32, axis=1)
    to_modes = np.tile(np.repeat(eye32, 16, axis=1), (4, 1))
    from_modes = to_modes.T.reshape(4, 128, 128)
    rows = np.repeat(eye32, XB, axis=0)
    lanes = np.tile(rows, (1, 4))
    return dict(
        wide_t=wide.T.copy(),
        bx=three(basis),
        wide=wide,
        bz=three(basis_z),
        spread=np.concatenate([spread, spread], axis=0),
        to_modes=np.concatenate([to_modes, to_modes], axis=0),
        bzt=three(basis_z.T),
        bxt=three(basis.T),
        rows=rows,
        rows_t=rows.T.copy(),
        lanes=lanes,
        from_modes=np.concatenate([from_modes, from_modes], axis=1),
        gather=np.concatenate([spread.T, spread.T], axis=0),
    )


TABLES = {name: np.asarray(table).astype(ml_dtypes.bfloat16) for name, table in tables().items()}
NAMES = tuple(TABLES)


def split(value):
    high = value.astype(BF)
    return high, (value - high.astype(F32)).astype(BF)


def dot(a, b):
    return jnp.dot(a, b, preferred_element_type=F32)


def dot_nt(a, b):
    return lax.dot_general(a, b, (((1,), (1,)), ((), ())), preferred_element_type=F32)


def dot_three(table, value):
    high, low = split(value)
    return dot(table, jnp.concatenate([high, low, high], axis=0))


def middle_out(at, size):
    return size // 2 + (at + 1) // 2 * (2 * lax.rem(at + 1, 2) - 1)


def far_first(me, at):
    x = lax.rem(me // 16 + middle_out(lax.rem(at // 2, 4), 4), 4)
    z = lax.rem(lax.rem(me // 2, 8) + middle_out(at // 8, 8), 8)
    return x * 16 + z * 2 + lax.rem(me + 1 + at, 2)


def kernel(n_slab, n_ens, field, weight, lw, bias, cot, *rest):
    consts = dict(zip(NAMES, rest[: len(NAMES)]))
    rest = rest[len(NAMES) :]
    out_v, gs_v, pre, s2, total_out = rest[:5]
    rest = rest[5:]
    tab = dict(zip(NAMES, rest[: len(NAMES)]))
    rest = rest[len(NAMES) :]
    (
        field_v, cot_v, w_v, slope_v, kl_f, kl_b, cexp, gacc,
        send, recv, call, ball, sums,
        load_sem, tab_sem, send_sem, recv_sem, ens_send, ens_recv, sum_send, sum_recv,
    ) = rest
    me = lax.axis_index("slab")
    mine = lax.axis_index("ens")
    x, z, core = me // 16, lax.rem(me // 2, 8), lax.rem(me, 2)

    barrier = pltpu.get_barrier_semaphore()

    def greet(at, carry):
        pl.semaphore_signal(barrier, inc=1, device_id={"slab": lax.rem(me + at, n_slab)}, device_id_type=MESH)
        return carry

    lax.fori_loop(1, n_slab, greet, 0)
    for at in range(1, n_ens):
        pl.semaphore_signal(barrier, inc=1, device_id={"ens": lax.rem(mine + at, n_ens)}, device_id_type=MESH)

    loads = [
        pltpu.make_async_copy(field, field_v, load_sem.at[0]),
        pltpu.make_async_copy(cot, cot_v, load_sem.at[1]),
        pltpu.make_async_copy(weight, w_v, load_sem.at[2]),
    ]
    tab_loads = {
        name: pltpu.make_async_copy(consts[name], tab[name], tab_sem.at[at])
        for at, name in enumerate(NAMES)
    }
    tab_loads["wide_t"].start()
    loads[0].start()
    for name in NAMES[1:]:
        tab_loads[name].start()
    loads[1].start()
    loads[2].start()

    def project(data, pair):
        return dot(jnp.concatenate(data, axis=1), tab["wide_t"][pair * 256 : (pair + 1) * 256, :])

    def exchange(phase):
        def one(at, carry):
            peer = far_first(me, at)
            pltpu.make_async_remote_copy(
                src_ref=send.at[phase, slot(peer)],
                dst_ref=recv.at[phase, slot(me)],
                send_sem=send_sem.at[phase],
                recv_sem=recv_sem.at[phase],
                device_id={"slab": peer},
                device_id_type=MESH,
            ).start()
            return carry

        lax.fori_loop(0, n_slab - 1, one, 0)
        recv[phase, slot(me)] = send[phase, slot(me)]

    def share(source, target, at_sem):
        for at in range(1, n_ens):
            pltpu.make_async_remote_copy(
                src_ref=source,
                dst_ref=target,
                send_sem=ens_send.at[at_sem],
                recv_sem=ens_recv.at[at_sem],
                device_id={"ens": lax.rem(mine + at, n_ens)},
                device_id_type=MESH,
            ).start()

    def wait_share(ref, at_sem):
        some = ref.at[pl.ds(0, n_ens - 1)]
        pltpu.make_async_copy(some, some, ens_recv.at[at_sem]).wait()

    def wait_share_sent(ref, at_sem):
        some = ref.at[pl.ds(0, n_ens - 1)]
        pltpu.make_async_copy(some, some, ens_send.at[at_sem]).wait()

    def share_sums(stage, place, peers):
        for peer in peers:
            pltpu.make_async_remote_copy(
                src_ref=sums.at[stage, place],
                dst_ref=sums.at[stage, place],
                send_sem=sum_send.at[stage],
                recv_sem=sum_recv.at[stage],
                device_id=peer,
                device_id_type=MESH,
            ).start()

    def wait_sums(stage, size, sem):
        some = sums.at[stage, pl.ds(0, size - 1)]
        pltpu.make_async_copy(some, some, sem.at[stage]).wait()

    def owned(phase):
        planes = jnp.concatenate([recv[phase, :, g, :] for g in range(4)], axis=1)
        return dot_three(tab["bz"][...], planes)

    def planes_out(phase, modes):
        planes = dot_three(tab["bzt"][...], modes)
        for g in range(4):
            send[phase, :, g, :] = planes[:, g * 128 : (g + 1) * 128]

    def own_pair(chunk, lanes):
        row = lax.broadcasted_iota(jnp.int32, (128, lanes), 0) // 32 + chunk * 4
        lane = lax.rem(lax.broadcasted_iota(jnp.int32, (128, lanes), 1), 16)
        return row == lane

    def masked(modes, keep):
        tall = jnp.concatenate([modes] * 4, axis=0)
        high, low = split(jnp.where(keep, tall, 0.0))
        return jnp.concatenate([high, low], axis=1)

    def fold(value, keep):
        value = jnp.where(keep, value, 0.0)
        return value[0:32] + value[32:64] + value[64:96] + value[96:128]

    def to_channels(modes, keep):
        total = None
        for g in range(4):
            part = dot(masked(modes[:, g * 128 : (g + 1) * 128], keep), tab["from_modes"][g])
            total = part if total is None else total + part
        return total

    def weights_of(chunk, g):
        return w_v[pl.ds(chunk * 4, 4), :, g * 256 : (g + 1) * 256].reshape(128, 256).astype(F32)

    def narrow(phase, g):
        modes = jnp.concatenate([recv[phase, :32, g, :], recv[phase, 32:, g, :]], axis=1)
        return dot_three(tab["bxt"][...], modes).astype(BF)

    def put(phase, g, total):
        modes = dot_three(tab["bx"][...], total)
        send[phase, :32, g, :] = modes[:, :128]
        send[phase, 32:, g, :] = modes[:, 128:]

    def block_of(ref, at):
        a = ref[:, pl.ds(pl.multiple_of(at * 2 * XB, 2 * XB), XB), :].reshape(C * XB, N)
        b = ref[:, pl.ds(pl.multiple_of(at * 2 * XB + XB, XB), XB), :].reshape(C * XB, N)
        return jnp.concatenate([a, b], axis=1)

    def pointwise(matrix, data):
        def step(at, carry):
            value = dot(matrix[...], block_of(data, at))
            pre[:, pl.ds(pl.multiple_of(at * 2 * XB, 2 * XB), XB), :] = value[:, :N].reshape(C, XB, N)
            pre[:, pl.ds(pl.multiple_of(at * 2 * XB + XB, XB), XB), :] = value[:, N:].reshape(C, XB, N)
            return carry

        lax.fori_loop(0, N // (2 * XB), step, 0)

    tab_loads["wide_t"].wait()
    tab_loads["bx"].wait()
    loads[0].wait()
    for g in range(4):
        total = None
        for pair in range(4):
            at = g * 8 + pair * 2
            part = project([field_v[at], field_v[at + 1]], pair)
            total = part if total is None else total + part
        put(0, g, total)
    pl.semaphore_wait(barrier, n_slab - 1 + n_ens - 1)
    exchange(0)

    for name in NAMES[2:]:
        tab_loads[name].wait()
    loads[1].wait()
    loads[2].wait()
    tall = dot(dot_nt(tab["rows"][...], lw[...]).astype(BF), tab["rows_t"][...])
    same = lax.rem(lax.broadcasted_iota(jnp.int32, (512, 512), 0), XB) == lax.rem(
        lax.broadcasted_iota(jnp.int32, (512, 512), 1), XB
    )
    kl_f[...] = jnp.where(same, tall, 0.0).astype(BF)
    tall = dot(dot(tab["rows"][...], lw[...]).astype(BF), tab["rows_t"][...])
    kl_b[...] = jnp.where(same, tall, 0.0).astype(BF)
    pointwise(kl_f, field_v)

    wait_all(recv, recv_sem, 0)
    coefs = owned(0)
    call[mine] = coefs

    def mix(chunk, total):
        keep = own_pair(chunk, 128)
        part = None
        for g in range(4):
            wide = dot(masked(coefs_at(call, mine, g), keep), tab["spread"][...])
            value = wide * weights_of(chunk, g)
            value = value[:, :128] + value[:, 128:]
            part = value if part is None else part + value
        high, low = split(part)
        value = dot(jnp.concatenate([high, low], axis=1), tab["to_modes"][...])
        return total + fold(value, own_pair(chunk, 512))

    mixed = lax.fori_loop(0, 4, mix, jnp.zeros((K, 512), F32), unroll=True)
    planes_out(1, mixed)
    exchange(1)


    def spread_member(at, carry):
        member = lax.rem(mine + at, n_ens)
        for chunk in range(4):
            keep = own_pair(chunk, 128)
            for g in range(4):
                cexp[member, chunk * 128 : (chunk + 1) * 128, g * 256 : (g + 1) * 256] = dot(
                    masked(coefs_at(call, member, g), keep), tab["spread"][...]
                )
        return carry

    spread_member(0, 0)

    wait_all(recv, recv_sem, 1)
    share(call.at[mine], call.at[mine], 0)
    for g in range(4):
        narrowed = narrow(1, g)
        total = None
        for pair in range(4):
            both = dot(narrowed, tab["wide"][:, pair * 256 : (pair + 1) * 256])
            slopes = []
            for half in range(2):
                o = g * 8 + pair * 2 + half
                v = both[:, half * 128 : (half + 1) * 128] + (pre[o] + bias[o])
                cubic = (ROOT * 0.044715) * (v * v)
                t = jnp.tanh(v * (ROOT + cubic))
                h = 0.5 * v
                out_v[o] = (h + h * t).astype(BF)
                grad = (0.5 + 0.5 * t) + (h * (1.0 - t * t)) * (ROOT + 3.0 * cubic)
                slopes.append((cot_v[o].astype(F32) * grad).astype(BF))
                slope_v[o] = slopes[-1]
            part = project(slopes, pair)
            total = part if total is None else total + part
        put(2, g, total)
    exchange(2)

    gacc[...] = jnp.zeros_like(gacc)

    def outer(at, carry):
        ones = jnp.ones((XB, 2 * N), BF)
        gacc[...] += dot_nt(jnp.concatenate([block_of(field_v, at), ones], axis=0), block_of(slope_v, at))
        return carry

    lax.fori_loop(0, N // (2 * XB), outer, 0)
    same = lax.rem(lax.broadcasted_iota(jnp.int32, (512, 512), 0), XB) == lax.rem(
        lax.broadcasted_iota(jnp.int32, (512, 512), 1), XB
    )
    rows = jnp.sum(jnp.where(same, gacc[: C * XB], 0.0).reshape(C, XB, 512), axis=1)
    bias_rows = gacc[C * XB : C * XB + XB]
    high, low = split(jnp.concatenate([rows, bias_rows], axis=0))
    rows = dot(high, tab["lanes"][...]) + dot(low, tab["lanes"][...])
    lane = lax.broadcasted_iota(jnp.int32, (8, 128), 1) // 32
    packed = jnp.zeros((8, 128), F32)
    for part in range(4):
        packed = packed + jnp.where(lane == part, rows[part * 8 : (part + 1) * 8], 0.0)
    near = x * 2 + core
    sums[0, near, :8] = packed
    sums[0, near, 8:] = rows[C : C + 8]
    peers = [lax.rem(near + at, 8) for at in range(1, 8)]
    share_sums(0, near, [{"slab": peer // 2 * 16 + z * 2 + lax.rem(peer, 2)} for peer in peers])
    pointwise(kl_b, slope_v)
    wait_share(call, 0)
    lax.fori_loop(1, n_ens, spread_member, 0)
    wait_sums(0, 8, sum_recv)
    sums[1, z] = jnp.sum(sums[0], axis=0)
    share_sums(1, z, [{"slab": x * 16 + lax.rem(z + at, 8) * 2 + core} for at in range(1, 8)])

    wait_all(recv, recv_sem, 2)
    back = owned(2)
    ball[mine] = back
    share(ball.at[mine], ball.at[mine], 1)

    def mix_back(chunk, total):
        keep = own_pair(chunk, 128)
        four = to_channels(ball[mine], keep)
        four = jnp.concatenate([four, four], axis=1)
        parts = []
        for g in range(4):
            high, low = split(weights_of(chunk, g) * four)
            value = dot(jnp.concatenate([high, low], axis=1), tab["gather"][...])
            parts.append(fold(value, keep))
        return total + jnp.concatenate(parts, axis=1)

    back_modes = lax.fori_loop(0, 4, mix_back, jnp.zeros((K, 512), F32), unroll=True)
    planes_out(3, back_modes)
    exchange(3)


    wait_sums(1, 8, sum_recv)
    sums[2, mine] = jnp.sum(sums[1], axis=0)
    share_sums(2, mine, [{"ens": lax.rem(mine + at, n_ens)} for at in range(1, n_ens)])
    wait_share(ball, 1)

    def spectral(chunk, carry):
        keep = own_pair(chunk, 128)
        rows = pl.ds(pl.multiple_of(chunk * 128, 128), 128)
        fours = []
        for member in range(n_ens):
            four = to_channels(ball[member], keep)
            fours.append(jnp.concatenate([four, four], axis=1))
        for g in range(4):
            total = None
            for member in range(n_ens):
                part = cexp[member, rows, g * 256 : (g + 1) * 256] * fours[member]
                total = part if total is None else total + part
            gs_v[pl.ds(chunk * 4, 4), :, g * 256 : (g + 1) * 256] = total.reshape(4, 32, 256)
        return carry

    lax.fori_loop(0, 4, spectral, 0)

    wait_all(recv, recv_sem, 3)
    for g in range(4):
        s2[g] = narrow(3, g)
    wait_sums(2, n_ens, sum_recv)
    total_out[...] = sums[2, 0] + sums[2, 1] + sums[2, 2] + sums[2, 3]

    for phase in range(4):
        wait_all(send, send_sem, phase)
    for stage, size in enumerate((8, 8, n_ens)):
        wait_sums(stage, size, sum_send)
    wait_share_sent(call, 0)
    wait_share_sent(ball, 1)


def finish_kernel(out_v, gs_v, pre, s2, total, wide, out, gf, gs, gl_out, gb_out, gf_v, sems):
    stores = [pltpu.make_async_copy(out_v, out, sems.at[4]), pltpu.make_async_copy(gs_v, gs, sems.at[5])]
    for store in stores:
        store.start()
    for g in range(4):
        for pair in range(4):
            both = dot(s2[g], wide[:, pair * 256 : (pair + 1) * 256])
            for half in range(2):
                o = g * 8 + pair * 2 + half
                gf_v[o] = (both[:, half * 128 : (half + 1) * 128] + pre[o]).astype(BF)
        some = pl.ds(g * 8, 8)
        stores.append(pltpu.make_async_copy(gf_v.at[some], gf.at[some], sems.at[g]))
        stores[-1].start()
    for part in range(4):
        gl_out[part * 8 : (part + 1) * 8, :] = total[:8, part * 32 : (part + 1) * 32]
    gb_out[...] = total[8:9, :32]
    for store in stores:
        store.wait()


def slot(device):
    return lax.rem(device, 2) * 32 + device // 2


def coefs_at(ref, member, g):
    return ref[member, :, g * 128 : (g + 1) * 128]


def wait_all(ref, sem, phase):
    some = ref.at[phase, pl.ds(0, NZ - 1)]
    pltpu.make_async_copy(some, some, sem.at[phase]).wait()


def local(n_slab, n_ens, field, weight, local_weight, bias, cotangent):
    consts = [jnp.asarray(TABLES[name]) for name in NAMES]
    any_spec = pl.BlockSpec(memory_space=pl.ANY)
    vmem = pl.BlockSpec(memory_space=pltpu.VMEM)
    smem = pl.BlockSpec(memory_space=pltpu.SMEM)
    image = (C, N, N)
    dma = pltpu.SemaphoreType.DMA
    held = pl.pallas_call(
        functools.partial(kernel, n_slab, n_ens),
        out_shape=(
            pltpu.VMEM(image, BF),
            pltpu.VMEM((16, 32, 1024), F32),
            pltpu.VMEM(image, F32),
            pltpu.VMEM((4, 128, 256), BF),
            pltpu.VMEM((16, 128), F32),
        ),
        in_specs=[any_spec, any_spec, vmem, smem, any_spec] + [any_spec] * len(NAMES),
        out_specs=(vmem,) * 5,
        scratch_shapes=[pltpu.VMEM(TABLES[name].shape, BF) for name in NAMES]
        + [
            pltpu.VMEM(image, BF),
            pltpu.VMEM(image, BF),
            pltpu.VMEM((16, 32, 1024), BF),
            pltpu.VMEM(image, BF),
            pltpu.VMEM((512, 512), BF),
            pltpu.VMEM((512, 512), BF),
            pltpu.VMEM((n_ens, 512, 1024), F32),
            pltpu.VMEM((512 + XB, 512), F32),
            pltpu.VMEM((4, NZ, 4, 128), F32),
            pltpu.VMEM((4, NZ, 4, 128), F32),
            pltpu.VMEM((n_ens, K, 512), F32),
            pltpu.VMEM((n_ens, K, 512), F32),
            pltpu.VMEM((3, 8, 16, 128), F32),
            dma((3,)),
            dma((len(NAMES),)),
            dma((4,)),
            dma((4,)),
            dma((2,)),
            dma((2,)),
            dma((3,)),
            dma((3,)),
        ],
        compiler_params=pltpu.CompilerParams(
            collective_id=0, has_side_effects=True, vmem_limit_bytes=57 * 1024 * 1024
        ),
    )(
        field.reshape(image),
        weight,
        local_weight,
        bias,
        cotangent.reshape(image),
        *consts,
    )
    held = [pltpu.with_memory_space_constraint(value, pltpu.VMEM) for value in (*held, consts[NAMES.index("wide")])]
    output, grad_field, grad_spectral, grad_local, grad_bias = pl.pallas_call(
        finish_kernel,
        out_shape=(
            jax.ShapeDtypeStruct(image, BF),
            jax.ShapeDtypeStruct(image, BF),
            jax.ShapeDtypeStruct((16, 32, 1024), F32),
            jax.ShapeDtypeStruct((32, 32), F32),
            jax.ShapeDtypeStruct((1, 32), F32),
        ),
        in_specs=[vmem] * 6,
        out_specs=(any_spec, any_spec, any_spec, vmem, vmem),
        scratch_shapes=[pltpu.VMEM(image, BF), dma((6,))],
        compiler_params=pltpu.CompilerParams(vmem_limit_bytes=16 * 1024 * 1024),
    )(*held)
    whole = (1, 1) + image
    return (
        output.reshape(whole),
        grad_field.reshape(whole),
        grad_spectral,
        grad_local,
        grad_bias.reshape(32),
    )


def solution(mesh):
    placed = (
        P("ens", "slab", None, None, None),
        P("slab", None, None),
        P(),
        P(),
        P("ens", "slab", None, None, None),
    )
    return jax.shard_map(
        functools.partial(local, mesh.shape["slab"], mesh.shape["ens"]),
        mesh=mesh,
        in_specs=placed,
        out_specs=(
            P("ens", "slab", None, None, None),
            P("ens", "slab", None, None, None),
            P("slab", None, None),
            P(),
            P(),
        ),
        check_vma=False,
    )
```

```python
import functools
import math

import jax
import jax.numpy as jnp
import ml_dtypes
import numpy as np
from jax import lax
from jax.experimental import pallas as pl
from jax.experimental.pallas import tpu as pltpu
from jax.sharding import PartitionSpec as P

BF = jnp.bfloat16
F32 = jnp.float32
MESH = pl.DeviceIdType.MESH
C = 32
N = 128
K = 32
NZ = 64
XB = 16
ROOT = math.sqrt(2.0 / math.pi)


def basis_table(modes, length):
    frequency = np.arange(modes, dtype=np.int32) - modes // 2
    points = np.arange(length, dtype=np.int32)
    product = frequency[:, None] * points[None, :] % length
    angles = product.astype(np.float32) * np.float32(2.0 * math.pi / length)
    return (np.cos(angles) + np.sin(angles)) / np.float32(math.sqrt(length))


def split_table(table):
    high = table.astype(ml_dtypes.bfloat16)
    low = (table - high.astype(np.float32)).astype(ml_dtypes.bfloat16)
    return high, low


def three(table):
    high, low = split_table(table)
    return np.concatenate([high, high, low], axis=1)


def tables():
    basis = basis_table(K, N)
    slots = np.arange(NZ)
    basis_z = basis_table(K, NZ)[:, slots % 32 * 2 + slots // 32]

    def widen(table):
        wide = np.zeros((2, 8, 16, 8, N), np.float32)
        for c in range(8):
            wide[:, c, :, c, :] = table.astype(np.float32).reshape(2, 16, N)
        return wide.reshape(256, 8 * N)

    high, low = (widen(table) for table in split_table(basis))
    eye8, eye32 = np.eye(8, dtype=np.float32), np.eye(32, dtype=np.float32)
    spread = np.repeat(np.repeat(eye8, 16, axis=0), 32, axis=1)
    to_modes = np.tile(np.repeat(eye32, 16, axis=1), (4, 1))
    from_modes = to_modes.T.reshape(4, 128, 128)
    rows = np.repeat(eye32, XB, axis=0)
    lanes = np.tile(rows, (1, 4))
    return dict(
        wide_t=high.T.copy(),
        bx=three(basis),
        wide=np.concatenate([high, high, low], axis=0),
        bz=three(basis_z),
        spread=np.concatenate([spread, spread], axis=0),
        to_modes=np.concatenate([to_modes, to_modes], axis=0),
        bzt=three(basis_z.T),
        bxt=three(basis.T),
        rows=rows,
        rows_t=rows.T.copy(),
        lanes=lanes,
        from_modes=np.concatenate([from_modes, from_modes], axis=1),
        gather=spread.T.copy(),
    )


TABLES = {name: np.asarray(table).astype(ml_dtypes.bfloat16) for name, table in tables().items()}
NAMES = tuple(TABLES)
WIDE = TABLES["wide"][:256]


def split(value):
    high = value.astype(BF)
    return high, (value - high.astype(F32)).astype(BF)


def dot(a, b):
    return jnp.dot(a, b, preferred_element_type=F32)


def dot_nt(a, b):
    return lax.dot_general(a, b, (((1,), (1,)), ((), ())), preferred_element_type=F32)


def dot_three(table, value):
    high, low = split(value)
    return dot(table, jnp.concatenate([high, low, high], axis=0))


def middle_out(at, size):
    return size // 2 + (at + 1) // 2 * (2 * lax.rem(at + 1, 2) - 1)


def far_first(me, at):
    x = lax.rem(me // 16 + middle_out(lax.rem(at // 2, 4), 4), 4)
    z = lax.rem(lax.rem(me // 2, 8) + middle_out(at // 8, 8), 8)
    return x * 16 + z * 2 + lax.rem(me + 1 + at, 2)


def kernel(n_slab, n_ens, field, weight, lw, bias, cot, *rest):
    consts = dict(zip(NAMES, rest[: len(NAMES)]))
    rest = rest[len(NAMES) :]
    out_v, gs_v, pre, s2, total_out = rest[:5]
    rest = rest[5:]
    tab = dict(zip(NAMES, rest[: len(NAMES)]))
    rest = rest[len(NAMES) :]
    (
        field_v, cot_v, w_v, slope_v, kl_f, kl_b, cexp, gacc,
        send, recv, call, ball, sums,
        load_sem, tab_sem, send_sem, recv_sem, ens_send, ens_recv, sum_send, sum_recv,
    ) = rest
    me = lax.axis_index("slab")
    mine = lax.axis_index("ens")
    x, z, core = me // 16, lax.rem(me // 2, 8), lax.rem(me, 2)

    barrier = pltpu.get_barrier_semaphore()

    def greet(at, carry):
        pl.semaphore_signal(barrier, inc=1, device_id={"slab": lax.rem(me + at, n_slab)}, device_id_type=MESH)
        return carry

    lax.fori_loop(1, n_slab, greet, 0)
    for at in range(1, n_ens):
        pl.semaphore_signal(barrier, inc=1, device_id={"ens": lax.rem(mine + at, n_ens)}, device_id_type=MESH)

    loads = [
        pltpu.make_async_copy(field, field_v, load_sem.at[0]),
        pltpu.make_async_copy(cot, cot_v, load_sem.at[1]),
        pltpu.make_async_copy(weight, w_v, load_sem.at[2]),
    ]
    tab_loads = {
        name: pltpu.make_async_copy(consts[name], tab[name], tab_sem.at[at])
        for at, name in enumerate(NAMES)
    }
    tab_loads["wide_t"].start()
    loads[0].start()
    for name in NAMES[1:]:
        tab_loads[name].start()
    loads[1].start()
    loads[2].start()

    def project(data, pair):
        tall = jnp.concatenate([jnp.concatenate(both, axis=1) for both in data], axis=0)
        return dot(tall, tab["wide_t"][pair * 256 : (pair + 1) * 256, :])

    def exchange(phase):
        def one(at, carry):
            peer = far_first(me, at)
            pltpu.make_async_remote_copy(
                src_ref=send.at[phase, slot(peer)],
                dst_ref=recv.at[phase, slot(me)],
                send_sem=send_sem.at[phase],
                recv_sem=recv_sem.at[phase],
                device_id={"slab": peer},
                device_id_type=MESH,
            ).start()
            return carry

        lax.fori_loop(0, n_slab - 1, one, 0)
        recv[phase, slot(me)] = send[phase, slot(me)]

    def share(source, target, at_sem):
        for at in range(1, n_ens):
            pltpu.make_async_remote_copy(
                src_ref=source,
                dst_ref=target,
                send_sem=ens_send.at[at_sem],
                recv_sem=ens_recv.at[at_sem],
                device_id={"ens": lax.rem(mine + at, n_ens)},
                device_id_type=MESH,
            ).start()

    def wait_share(ref, at_sem):
        some = ref.at[pl.ds(0, n_ens - 1)]
        pltpu.make_async_copy(some, some, ens_recv.at[at_sem]).wait()

    def wait_share_sent(ref, at_sem):
        some = ref.at[pl.ds(0, n_ens - 1)]
        pltpu.make_async_copy(some, some, ens_send.at[at_sem]).wait()

    def share_sums(stage, place, peers):
        for peer in peers:
            pltpu.make_async_remote_copy(
                src_ref=sums.at[stage, place],
                dst_ref=sums.at[stage, place],
                send_sem=sum_send.at[stage],
                recv_sem=sum_recv.at[stage],
                device_id=peer,
                device_id_type=MESH,
            ).start()

    def wait_sums(stage, size, sem):
        some = sums.at[stage, pl.ds(0, size - 1)]
        pltpu.make_async_copy(some, some, sem.at[stage]).wait()

    def owned(phase):
        planes = jnp.concatenate([recv[phase, :, g, :] for g in range(4)], axis=1)
        return dot_three(tab["bz"][...], planes)

    def planes_out(phase, modes):
        planes = dot_three(tab["bzt"][...], modes)
        for g in range(4):
            send[phase, :, g, :] = planes[:, g * 128 : (g + 1) * 128]

    def own_pair(chunk, lanes):
        row = lax.broadcasted_iota(jnp.int32, (128, lanes), 0) // 32 + chunk * 4
        lane = lax.rem(lax.broadcasted_iota(jnp.int32, (128, lanes), 1), 16)
        return row == lane

    def masked(modes, keep):
        tall = jnp.concatenate([modes] * 4, axis=0)
        high, low = split(jnp.where(keep, tall, 0.0))
        return jnp.concatenate([high, low], axis=1)

    def to_channels(modes, keep):
        total = None
        for g in range(4):
            part = dot(masked(modes[:, g * 128 : (g + 1) * 128], keep), tab["from_modes"][g])
            total = part if total is None else total + part
        return total

    def own_pair_all(lanes):
        row = lax.broadcasted_iota(jnp.int32, (512, lanes), 0) // 32
        return row == lax.rem(lax.broadcasted_iota(jnp.int32, (512, lanes), 1), 16)

    def fold_all(value, keep):
        return jnp.sum(jnp.where(keep, value, 0.0).reshape(16, 32, value.shape[1]), axis=0)

    def weights_all(g):
        return w_v[:, :, g * 256 : (g + 1) * 256].reshape(512, 256).astype(F32)

    def narrow(phase, g):
        modes = jnp.concatenate([recv[phase, :32, g, :], recv[phase, 32:, g, :]], axis=1)
        return dot_three(tab["bxt"][...], modes)

    def put(phase, total):
        for g in range(4):
            modes = dot_three(tab["bx"][...], total[g * 128 : (g + 1) * 128])
            send[phase, :32, g, :] = modes[:, :128]
            send[phase, 32:, g, :] = modes[:, 128:]

    def block_of(ref, at):
        a = ref[:, pl.ds(pl.multiple_of(at * 2 * XB, 2 * XB), XB), :].reshape(C * XB, N)
        b = ref[:, pl.ds(pl.multiple_of(at * 2 * XB + XB, XB), XB), :].reshape(C * XB, N)
        return jnp.concatenate([a, b], axis=1)

    def pointwise(matrix, data):
        def step(at, carry):
            value = dot(matrix[...], block_of(data, at))
            pre[:, pl.ds(pl.multiple_of(at * 2 * XB, 2 * XB), XB), :] = value[:, :N].reshape(C, XB, N)
            pre[:, pl.ds(pl.multiple_of(at * 2 * XB + XB, XB), XB), :] = value[:, N:].reshape(C, XB, N)
            return carry

        lax.fori_loop(0, N // (2 * XB), step, 0)

    tab_loads["wide_t"].wait()
    tab_loads["bx"].wait()
    loads[0].wait()
    total = None
    for pair in range(4):
        part = project([[field_v[g * 8 + pair * 2 + half] for half in range(2)] for g in range(4)], pair)
        total = part if total is None else total + part
    put(0, total)
    pl.semaphore_wait(barrier, n_slab - 1 + n_ens - 1)
    exchange(0)

    for name in NAMES[2:]:
        tab_loads[name].wait()
    loads[1].wait()
    loads[2].wait()
    tall = dot(dot_nt(tab["rows"][...], lw[...]).astype(BF), tab["rows_t"][...])
    same = lax.rem(lax.broadcasted_iota(jnp.int32, (512, 512), 0), XB) == lax.rem(
        lax.broadcasted_iota(jnp.int32, (512, 512), 1), XB
    )
    kl_f[...] = jnp.where(same, tall, 0.0).astype(BF)
    tall = dot(dot(tab["rows"][...], lw[...]).astype(BF), tab["rows_t"][...])
    kl_b[...] = jnp.where(same, tall, 0.0).astype(BF)
    pointwise(kl_f, field_v)

    def add_bias(o, carry):
        pre[o] = pre[o] + bias[o]
        return carry

    lax.fori_loop(0, C, add_bias, 0)

    wait_all(recv, recv_sem, 0)
    coefs = owned(0)
    call[mine] = coefs

    own, own_wide = own_pair_all(128), own_pair_all(512)
    part = None
    for g in range(4):
        high, low = split(jnp.where(own, jnp.concatenate([coefs[:, g * 128 : (g + 1) * 128]] * 16, axis=0), 0.0))
        value = dot(jnp.concatenate([high, low], axis=1), tab["spread"][...]) * weights_all(g)
        value = value[:, :128] + value[:, 128:]
        part = value if part is None else part + value
    high, low = split(part)
    mixed = fold_all(dot(jnp.concatenate([high, low], axis=1), tab["to_modes"][...]), own_wide)
    planes_out(1, mixed)
    exchange(1)


    def spread_member(at, carry):
        member = lax.rem(mine + at, n_ens)
        for chunk in range(4):
            keep = own_pair(chunk, 128)
            for g in range(4):
                cexp[member, chunk * 128 : (chunk + 1) * 128, g * 256 : (g + 1) * 256] = dot(
                    masked(coefs_at(call, member, g), keep), tab["spread"][...]
                )
        return carry

    spread_member(0, 0)

    wait_all(recv, recv_sem, 1)
    share(call.at[mine], call.at[mine], 0)
    narrowed = []
    for g in range(4):
        high, low = split(narrow(1, g))
        narrowed.append(jnp.concatenate([high, low, high], axis=1))
    narrowed = jnp.concatenate(narrowed, axis=0)
    total = None
    for pair in range(4):
        both = dot(narrowed, tab["wide"][:, pair * 256 : (pair + 1) * 256])
        slopes = []
        for g in range(4):
            slopes.append([])
            for half in range(2):
                o = g * 8 + pair * 2 + half
                v = both[g * 128 : (g + 1) * 128, half * 128 : (half + 1) * 128] + pre[o]
                cubic = (ROOT * 0.044715) * (v * v)
                t = jnp.tanh(v * (ROOT + cubic))
                h = 0.5 * v
                more = 1.0 + t
                out_v[o] = (h * more).astype(BF)
                grad = more * (0.5 + (h * (ROOT + 3.0 * cubic)) * (1.0 - t))
                slope = (cot_v[o].astype(F32) * grad).astype(BF)
                slope_v[o] = slope
                slopes[g].append(slope)
        part = project(slopes, pair)
        total = part if total is None else total + part
    put(2, total)

    exchange(2)

    gacc[...] = jnp.zeros_like(gacc)

    def outer(at, carry):
        ones = jnp.ones((XB, 2 * N), BF)
        gacc[...] += dot_nt(jnp.concatenate([block_of(field_v, at), ones], axis=0), block_of(slope_v, at))
        return carry

    lax.fori_loop(0, N // (2 * XB), outer, 0)
    same = lax.rem(lax.broadcasted_iota(jnp.int32, (512, 512), 0), XB) == lax.rem(
        lax.broadcasted_iota(jnp.int32, (512, 512), 1), XB
    )
    rows = jnp.sum(jnp.where(same, gacc[: C * XB], 0.0).reshape(C, XB, 512), axis=1)
    bias_rows = gacc[C * XB : C * XB + XB]
    high, low = split(jnp.concatenate([rows, bias_rows], axis=0))
    rows = dot(high, tab["lanes"][...]) + dot(low, tab["lanes"][...])
    lane = lax.broadcasted_iota(jnp.int32, (8, 128), 1) // 32
    packed = jnp.zeros((8, 128), F32)
    for part in range(4):
        packed = packed + jnp.where(lane == part, rows[part * 8 : (part + 1) * 8], 0.0)
    near = x * 2 + core
    sums[0, near, :8] = packed
    sums[0, near, 8:] = rows[C : C + 8]
    peers = [lax.rem(near + at, 8) for at in range(1, 8)]
    share_sums(0, near, [{"slab": peer // 2 * 16 + z * 2 + lax.rem(peer, 2)} for peer in peers])
    pointwise(kl_b, slope_v)
    wait_share(call, 0)
    lax.fori_loop(1, n_ens, spread_member, 0)
    wait_sums(0, 8, sum_recv)
    sums[1, z] = jnp.sum(sums[0], axis=0)
    share_sums(1, z, [{"slab": x * 16 + lax.rem(z + at, 8) * 2 + core} for at in range(1, 8)])

    wait_all(recv, recv_sem, 2)
    back = owned(2)
    ball[mine] = back
    share(ball.at[mine], ball.at[mine], 1)

    four = None
    for g in range(4):
        tall = jnp.concatenate([back[:, g * 128 : (g + 1) * 128]] * 16, axis=0)
        part = dot(jnp.where(own, tall, 0.0).astype(BF), tab["from_modes"][g, :128])
        four = part if four is None else four + part
    four = jnp.concatenate([four, four], axis=1)
    tall = jnp.concatenate([(weights_all(g) * four).astype(BF) for g in range(4)], axis=0)
    tall = dot(tall, tab["gather"][...])
    back_modes = jnp.concatenate([fold_all(tall[g * 512 : (g + 1) * 512], own) for g in range(4)], axis=1)
    planes_out(3, back_modes)
    exchange(3)


    wait_sums(1, 8, sum_recv)
    sums[2, mine] = jnp.sum(sums[1], axis=0)
    share_sums(2, mine, [{"ens": lax.rem(mine + at, n_ens)} for at in range(1, n_ens)])
    wait_share(ball, 1)

    def spectral(chunk, carry):
        keep = own_pair(chunk, 128)
        rows = pl.ds(pl.multiple_of(chunk * 128, 128), 128)
        fours = []
        for member in range(n_ens):
            four = to_channels(ball[member], keep)
            fours.append(jnp.concatenate([four, four], axis=1))
        for g in range(4):
            total = None
            for member in range(n_ens):
                part = cexp[member, rows, g * 256 : (g + 1) * 256] * fours[member]
                total = part if total is None else total + part
            gs_v[pl.ds(chunk * 4, 4), :, g * 256 : (g + 1) * 256] = total.reshape(4, 32, 256)
        return carry

    lax.fori_loop(0, 4, spectral, 0)

    wait_all(recv, recv_sem, 3)
    for g in range(4):
        s2[g * 128 : (g + 1) * 128] = narrow(3, g).astype(BF)
    wait_sums(2, n_ens, sum_recv)
    total_out[...] = sums[2, 0] + sums[2, 1] + sums[2, 2] + sums[2, 3]

    for phase in range(4):
        wait_all(send, send_sem, phase)
    for stage, size in enumerate((8, 8, n_ens)):
        wait_sums(stage, size, sum_send)
    wait_share_sent(call, 0)
    wait_share_sent(ball, 1)


def finish_kernel(out_v, gs_v, pre, s2, total, wide, out, gf, gs, gl_out, gb_out, gf_v, sems):
    stores = []
    for part in range(4):
        eight, four = pl.ds(part * 8, 8), pl.ds(part * 4, 4)
        stores.append(pltpu.make_async_copy(gs_v.at[four], gs.at[four], sems.at[part]))
        stores.append(pltpu.make_async_copy(out_v.at[eight], out.at[eight], sems.at[4 + part]))
    for store in stores:
        store.start()
    for pair in range(4):
        both = dot(s2[...], wide[:, pair * 256 : (pair + 1) * 256])
        for g in range(4):
            some = pl.ds(g * 8 + pair * 2, 2)
            for half in range(2):
                o = g * 8 + pair * 2 + half
                value = both[g * 128 : (g + 1) * 128, half * 128 : (half + 1) * 128]
                gf_v[o] = (value + pre[o]).astype(BF)
            stores.append(pltpu.make_async_copy(gf_v.at[some], gf.at[some], sems.at[8 + pair * 4 + g]))
            stores[-1].start()
    for part in range(4):
        gl_out[part * 8 : (part + 1) * 8, :] = total[:8, part * 32 : (part + 1) * 32]
    gb_out[...] = total[8:9, :32]
    for store in stores:
        store.wait()


def slot(device):
    return lax.rem(device, 2) * 32 + device // 2


def coefs_at(ref, member, g):
    return ref[member, :, g * 128 : (g + 1) * 128]


def wait_all(ref, sem, phase):
    some = ref.at[phase, pl.ds(0, NZ - 1)]
    pltpu.make_async_copy(some, some, sem.at[phase]).wait()


def local(n_slab, n_ens, field, weight, local_weight, bias, cotangent):
    consts = [jnp.asarray(TABLES[name]) for name in NAMES]
    any_spec = pl.BlockSpec(memory_space=pl.ANY)
    vmem = pl.BlockSpec(memory_space=pltpu.VMEM)
    smem = pl.BlockSpec(memory_space=pltpu.SMEM)
    image = (C, N, N)
    dma = pltpu.SemaphoreType.DMA
    held = pl.pallas_call(
        functools.partial(kernel, n_slab, n_ens),
        out_shape=(
            pltpu.VMEM(image, BF),
            pltpu.VMEM((16, 32, 1024), F32),
            pltpu.VMEM(image, F32),
            pltpu.VMEM((512, 256), BF),
            pltpu.VMEM((16, 128), F32),
        ),
        in_specs=[any_spec, any_spec, vmem, smem, any_spec] + [any_spec] * len(NAMES),
        out_specs=(vmem,) * 5,
        scratch_shapes=[pltpu.VMEM(TABLES[name].shape, BF) for name in NAMES]
        + [
            pltpu.VMEM(image, BF),
            pltpu.VMEM(image, BF),
            pltpu.VMEM((16, 32, 1024), BF),
            pltpu.VMEM(image, BF),
            pltpu.VMEM((512, 512), BF),
            pltpu.VMEM((512, 512), BF),
            pltpu.VMEM((n_ens, 512, 1024), F32),
            pltpu.VMEM((512 + XB, 512), F32),
            pltpu.VMEM((4, NZ, 4, 128), F32),
            pltpu.VMEM((4, NZ, 4, 128), F32),
            pltpu.VMEM((n_ens, K, 512), F32),
            pltpu.VMEM((n_ens, K, 512), F32),
            pltpu.VMEM((3, 8, 16, 128), F32),
            dma((3,)),
            dma((len(NAMES),)),
            dma((4,)),
            dma((4,)),
            dma((2,)),
            dma((2,)),
            dma((3,)),
            dma((3,)),
        ],
        compiler_params=pltpu.CompilerParams(
            collective_id=0, has_side_effects=True, vmem_limit_bytes=57 * 1024 * 1024
        ),
    )(
        field.reshape(image),
        weight,
        local_weight,
        bias,
        cotangent.reshape(image),
        *consts,
    )
    held = [pltpu.with_memory_space_constraint(value, pltpu.VMEM) for value in (*held, jnp.asarray(WIDE))]
    output, grad_field, grad_spectral, grad_local, grad_bias = pl.pallas_call(
        finish_kernel,
        out_shape=(
            jax.ShapeDtypeStruct(image, BF),
            jax.ShapeDtypeStruct(image, BF),
            jax.ShapeDtypeStruct((16, 32, 1024), F32),
            jax.ShapeDtypeStruct((32, 32), F32),
            jax.ShapeDtypeStruct((1, 32), F32),
        ),
        in_specs=[vmem] * 6,
        out_specs=(any_spec, any_spec, any_spec, vmem, vmem),
        scratch_shapes=[pltpu.VMEM(image, BF), dma((24,))],
        compiler_params=pltpu.CompilerParams(vmem_limit_bytes=16 * 1024 * 1024),
    )(*held)
    whole = (1, 1) + image
    return (
        output.reshape(whole),
        grad_field.reshape(whole),
        grad_spectral,
        grad_local,
        grad_bias.reshape(32),
    )


def solution(mesh):
    placed = (
        P("ens", "slab", None, None, None),
        P("slab", None, None),
        P(),
        P(),
        P("ens", "slab", None, None, None),
    )
    return jax.shard_map(
        functools.partial(local, mesh.shape["slab"], mesh.shape["ens"]),
        mesh=mesh,
        in_specs=placed,
        out_specs=(
            P("ens", "slab", None, None, None),
            P("ens", "slab", None, None, None),
            P("slab", None, None),
            P(),
            P(),
        ),
        check_vma=False,
    )
```

```python
import functools
import math

import jax
import jax.numpy as jnp
import ml_dtypes
import numpy as np
from jax import lax
from jax.experimental import pallas as pl
from jax.experimental.pallas import tpu as pltpu
from jax.sharding import PartitionSpec as P

BF = jnp.bfloat16
F32 = jnp.float32
MESH = pl.DeviceIdType.MESH
C = 32
N = 128
K = 32
NZ = 64
XB = 16
ROOT = math.sqrt(2.0 / math.pi)


def basis_table(modes, length):
    frequency = np.arange(modes, dtype=np.int32) - modes // 2
    points = np.arange(length, dtype=np.int32)
    product = frequency[:, None] * points[None, :] % length
    angles = product.astype(np.float32) * np.float32(2.0 * math.pi / length)
    return (np.cos(angles) + np.sin(angles)) / np.float32(math.sqrt(length))


def split_table(table):
    high = table.astype(ml_dtypes.bfloat16)
    low = (table - high.astype(np.float32)).astype(ml_dtypes.bfloat16)
    return high, low


def three(table):
    high, low = split_table(table)
    return np.concatenate([high, high, low], axis=1)


def tables():
    basis = basis_table(K, N)
    slots = np.arange(NZ)
    basis_z = basis_table(K, NZ)[:, slots % 32 * 2 + slots // 32]

    def widen(table):
        wide = np.zeros((2, 8, 16, 8, N), np.float32)
        for c in range(8):
            wide[:, c, :, c, :] = table.astype(np.float32).reshape(2, 16, N)
        return wide.reshape(256, 8 * N)

    high, low = (widen(table) for table in split_table(basis))
    eye8, eye32 = np.eye(8, dtype=np.float32), np.eye(32, dtype=np.float32)
    spread = np.repeat(np.repeat(eye8, 16, axis=0), 32, axis=1)
    to_modes = np.tile(np.repeat(eye32, 16, axis=1), (4, 1))
    from_modes = to_modes.T.reshape(4, 128, 128)
    rows = np.repeat(eye32, XB, axis=0)
    lanes = np.tile(rows, (1, 4))
    return dict(
        wide_t=high.T.copy(),
        bx=three(basis),
        wide=np.concatenate([high, high, low], axis=0),
        bz=three(basis_z),
        spread=np.concatenate([spread, spread], axis=0),
        to_modes=np.concatenate([to_modes, to_modes], axis=0),
        bzt=three(basis_z.T),
        bxt=three(basis.T),
        rows=rows,
        rows_t=rows.T.copy(),
        lanes=lanes,
        from_modes=np.concatenate([from_modes, from_modes], axis=1),
        gather=spread.T.copy(),
    )


TABLES = {name: np.asarray(table).astype(ml_dtypes.bfloat16) for name, table in tables().items()}
NAMES = tuple(TABLES)
WIDE = TABLES["wide"][:256]


def split(value):
    high = value.astype(BF)
    return high, (value - high.astype(F32)).astype(BF)


def dot(a, b):
    return jnp.dot(a, b, preferred_element_type=F32)


def dot_nt(a, b):
    return lax.dot_general(a, b, (((1,), (1,)), ((), ())), preferred_element_type=F32)


def dot_three(table, value):
    high, low = split(value)
    return dot(table, jnp.concatenate([high, low, high], axis=0))


def middle_out(at, size):
    return size // 2 + (at + 1) // 2 * (2 * lax.rem(at + 1, 2) - 1)


def kernel(n_slab, n_ens, field, weight, lw_in, bias_in, cot, *rest):
    consts = dict(zip(NAMES, rest[: len(NAMES)]))
    rest = rest[len(NAMES) :]
    out_v, gs_v, pre, s2, total_out = rest[:5]
    rest = rest[5:]
    tab = dict(zip(NAMES, rest[: len(NAMES)]))
    rest = rest[len(NAMES) :]
    (
        field_v, cot_v, w_v, lw, bias, slope_v, kl_f, kl_b, cexp, gacc,
        send, recv, call, ball, sums,
        load_sem, tab_sem, send_sem, recv_sem, ens_send, ens_recv, sum_send, sum_recv,
    ) = rest
    me = lax.axis_index("slab")
    mine = lax.axis_index("ens")
    x, z, core = me // 16, lax.rem(me // 2, 8), lax.rem(me, 2)
    my_slot = core * 32 + me // 2
    places = [(lax.rem(x + at, 4), lax.rem(core + 1 + other, 2)) for at in (2, 1, 3, 0) for other in range(2)]

    barrier = pltpu.get_barrier_semaphore()

    def greet(at, carry):
        pl.semaphore_signal(barrier, inc=1, device_id={"slab": lax.rem(me + at, n_slab)}, device_id_type=MESH)
        return carry

    lax.fori_loop(1, n_slab, greet, 0)
    for at in range(1, n_ens):
        pl.semaphore_signal(barrier, inc=1, device_id={"ens": lax.rem(mine + at, n_ens)}, device_id_type=MESH)

    loads = [
        pltpu.make_async_copy(field, field_v, load_sem.at[0]),
        pltpu.make_async_copy(cot, cot_v, load_sem.at[1]),
        pltpu.make_async_copy(weight, w_v, load_sem.at[2]),
        pltpu.make_async_copy(lw_in, lw, load_sem.at[3]),
        pltpu.make_async_copy(bias_in, bias, load_sem.at[4]),
    ]
    tab_loads = {
        name: pltpu.make_async_copy(consts[name], tab[name], tab_sem.at[at])
        for at, name in enumerate(NAMES)
    }
    tab_loads["wide_t"].start()
    loads[0].start()
    for name in NAMES[1:]:
        tab_loads[name].start()
    for load in loads[1:]:
        load.start()

    def project(data, pair):
        tall = jnp.concatenate([jnp.concatenate(both, axis=1) for both in data], axis=0)
        return dot(tall, tab["wide_t"][pair * 256 : (pair + 1) * 256, :])

    def exchange(phase):
        def one(to_x, to_z, to_core):
            pltpu.make_async_remote_copy(
                src_ref=send.at[phase, to_core * 32 + to_x * 8 + to_z],
                dst_ref=recv.at[phase, my_slot],
                send_sem=send_sem.at[phase],
                recv_sem=recv_sem.at[phase],
                device_id={"slab": to_x * 16 + to_z * 2 + to_core},
                device_id_type=MESH,
            ).start()

        def ring(at, carry):
            to_z = lax.rem(z + middle_out(at, 8), 8)
            for to_x, to_core in places:
                one(to_x, to_z, to_core)
            return carry

        lax.fori_loop(0, 7, ring, 0)
        for to_x, to_core in places[:-1]:
            one(to_x, z, to_core)
        recv[phase, my_slot] = send[phase, my_slot]

    def share(source, target, at_sem):
        for at in range(1, n_ens):
            pltpu.make_async_remote_copy(
                src_ref=source,
                dst_ref=target,
                send_sem=ens_send.at[at_sem],
                recv_sem=ens_recv.at[at_sem],
                device_id={"ens": lax.rem(mine + at, n_ens)},
                device_id_type=MESH,
            ).start()

    def wait_share(ref, at_sem):
        some = ref.at[pl.ds(0, n_ens - 1)]
        pltpu.make_async_copy(some, some, ens_recv.at[at_sem]).wait()

    def wait_share_sent(ref, at_sem):
        some = ref.at[pl.ds(0, n_ens - 1)]
        pltpu.make_async_copy(some, some, ens_send.at[at_sem]).wait()

    def share_sums(stage, place, peers):
        for peer in peers:
            pltpu.make_async_remote_copy(
                src_ref=sums.at[stage, place],
                dst_ref=sums.at[stage, place],
                send_sem=sum_send.at[stage],
                recv_sem=sum_recv.at[stage],
                device_id=peer,
                device_id_type=MESH,
            ).start()

    def wait_sums(stage, size, sem):
        some = sums.at[stage, pl.ds(0, size - 1)]
        pltpu.make_async_copy(some, some, sem.at[stage]).wait()

    def owned(phase):
        planes = jnp.concatenate([recv[phase, :, g, :] for g in range(4)], axis=1)
        return dot_three(tab["bz"][...], planes)

    def planes_out(phase, modes):
        planes = dot_three(tab["bzt"][...], modes)
        for g in range(4):
            send[phase, :, g, :] = planes[:, g * 128 : (g + 1) * 128]

    def own_pair(chunk, lanes):
        row = lax.broadcasted_iota(jnp.int32, (128, lanes), 0) // 32 + chunk * 4
        lane = lax.rem(lax.broadcasted_iota(jnp.int32, (128, lanes), 1), 16)
        return row == lane

    def masked(modes, keep):
        tall = jnp.concatenate([modes] * 4, axis=0)
        high, low = split(jnp.where(keep, tall, 0.0))
        return jnp.concatenate([high, low], axis=1)

    def to_channels(modes, keep):
        total = None
        for g in range(4):
            part = dot(masked(modes[:, g * 128 : (g + 1) * 128], keep), tab["from_modes"][g])
            total = part if total is None else total + part
        return total

    def own_pair_all(lanes):
        row = lax.broadcasted_iota(jnp.int32, (512, lanes), 0) // 32
        return row == lax.rem(lax.broadcasted_iota(jnp.int32, (512, lanes), 1), 16)

    def fold_all(value, keep):
        return jnp.sum(jnp.where(keep, value, 0.0).reshape(16, 32, value.shape[1]), axis=0)

    def weights_all(g):
        return w_v[:, :, g * 256 : (g + 1) * 256].reshape(512, 256).astype(F32)

    def narrow(phase, g):
        modes = jnp.concatenate([recv[phase, :32, g, :], recv[phase, 32:, g, :]], axis=1)
        return dot_three(tab["bxt"][...], modes)

    def put(phase, total):
        for g in range(4):
            modes = dot_three(tab["bx"][...], total[g * 128 : (g + 1) * 128])
            send[phase, :32, g, :] = modes[:, :128]
            send[phase, 32:, g, :] = modes[:, 128:]

    def block_of(ref, at):
        a = ref[:, pl.ds(pl.multiple_of(at * 2 * XB, 2 * XB), XB), :].reshape(C * XB, N)
        b = ref[:, pl.ds(pl.multiple_of(at * 2 * XB + XB, XB), XB), :].reshape(C * XB, N)
        return jnp.concatenate([a, b], axis=1)

    def pointwise(matrix, data):
        def step(at, carry):
            value = dot(matrix[...], block_of(data, at))
            pre[:, pl.ds(pl.multiple_of(at * 2 * XB, 2 * XB), XB), :] = value[:, :N].reshape(C, XB, N)
            pre[:, pl.ds(pl.multiple_of(at * 2 * XB + XB, XB), XB), :] = value[:, N:].reshape(C, XB, N)
            return carry

        lax.fori_loop(0, N // (2 * XB), step, 0)

    tab_loads["wide_t"].wait()
    tab_loads["bx"].wait()
    loads[0].wait()
    total = None
    for pair in range(4):
        part = project([[field_v[g * 8 + pair * 2 + half] for half in range(2)] for g in range(4)], pair)
        total = part if total is None else total + part
    put(0, total)
    pl.semaphore_wait(barrier, n_slab - 1 + n_ens - 1)
    exchange(0)

    for name in NAMES[2:]:
        tab_loads[name].wait()
    for load in loads[1:]:
        load.wait()
    tall = dot(dot_nt(tab["rows"][...], lw[...]).astype(BF), tab["rows_t"][...])
    same = lax.rem(lax.broadcasted_iota(jnp.int32, (512, 512), 0), XB) == lax.rem(
        lax.broadcasted_iota(jnp.int32, (512, 512), 1), XB
    )
    kl_f[...] = jnp.where(same, tall, 0.0).astype(BF)
    tall = dot(dot(tab["rows"][...], lw[...]).astype(BF), tab["rows_t"][...])
    kl_b[...] = jnp.where(same, tall, 0.0).astype(BF)
    pointwise(kl_f, field_v)

    def add_bias(o, carry):
        pre[o] = pre[o] + bias[o]
        return carry

    lax.fori_loop(0, C, add_bias, 0)

    wait_all(recv, recv_sem, 0)
    coefs = owned(0)
    call[mine] = coefs

    own, own_wide = own_pair_all(128), own_pair_all(512)
    part = None
    for g in range(4):
        high, low = split(jnp.where(own, jnp.concatenate([coefs[:, g * 128 : (g + 1) * 128]] * 16, axis=0), 0.0))
        value = dot(jnp.concatenate([high, low], axis=1), tab["spread"][...]) * weights_all(g)
        value = value[:, :128] + value[:, 128:]
        part = value if part is None else part + value
    high, low = split(part)
    mixed = fold_all(dot(jnp.concatenate([high, low], axis=1), tab["to_modes"][...]), own_wide)
    planes_out(1, mixed)
    exchange(1)


    def spread_member(at, carry):
        member = lax.rem(mine + at, n_ens)
        for chunk in range(4):
            keep = own_pair(chunk, 128)
            for g in range(4):
                cexp[member, chunk * 128 : (chunk + 1) * 128, g * 256 : (g + 1) * 256] = dot(
                    masked(coefs_at(call, member, g), keep), tab["spread"][...]
                )
        return carry

    spread_member(0, 0)

    wait_all(recv, recv_sem, 1)
    share(call.at[mine], call.at[mine], 0)
    narrowed = []
    for g in range(4):
        high, low = split(narrow(1, g))
        narrowed.append(jnp.concatenate([high, low, high], axis=1))
    narrowed = jnp.concatenate(narrowed, axis=0)
    total = None
    for pair in range(4):
        both = dot(narrowed, tab["wide"][:, pair * 256 : (pair + 1) * 256])
        slopes = []
        for g in range(4):
            slopes.append([])
            for half in range(2):
                o = g * 8 + pair * 2 + half
                v = both[g * 128 : (g + 1) * 128, half * 128 : (half + 1) * 128] + pre[o]
                cubic = (ROOT * 0.044715) * (v * v)
                t = jnp.tanh(v * (ROOT + cubic))
                h = 0.5 * v
                more = 1.0 + t
                out_v[o] = (h * more).astype(BF)
                grad = more * (0.5 + (h * (ROOT + 3.0 * cubic)) * (1.0 - t))
                slope = (cot_v[o].astype(F32) * grad).astype(BF)
                slope_v[o] = slope
                slopes[g].append(slope)
        part = project(slopes, pair)
        total = part if total is None else total + part
    put(2, total)

    exchange(2)

    gacc[...] = jnp.zeros_like(gacc)

    def outer(at, carry):
        ones = jnp.ones((XB, 2 * N), BF)
        gacc[...] += dot_nt(jnp.concatenate([block_of(field_v, at), ones], axis=0), block_of(slope_v, at))
        return carry

    lax.fori_loop(0, N // (2 * XB), outer, 0)
    same = lax.rem(lax.broadcasted_iota(jnp.int32, (512, 512), 0), XB) == lax.rem(
        lax.broadcasted_iota(jnp.int32, (512, 512), 1), XB
    )
    rows = jnp.sum(jnp.where(same, gacc[: C * XB], 0.0).reshape(C, XB, 512), axis=1)
    bias_rows = gacc[C * XB : C * XB + XB]
    high, low = split(jnp.concatenate([rows, bias_rows], axis=0))
    rows = dot(high, tab["lanes"][...]) + dot(low, tab["lanes"][...])
    lane = lax.broadcasted_iota(jnp.int32, (8, 128), 1) // 32
    packed = jnp.zeros((8, 128), F32)
    for part in range(4):
        packed = packed + jnp.where(lane == part, rows[part * 8 : (part + 1) * 8], 0.0)
    near = x * 2 + core
    sums[0, near, :8] = packed
    sums[0, near, 8:] = rows[C : C + 8]
    peers = [lax.rem(near + at, 8) for at in range(1, 8)]
    share_sums(0, near, [{"slab": peer // 2 * 16 + z * 2 + lax.rem(peer, 2)} for peer in peers])
    pointwise(kl_b, slope_v)
    wait_share(call, 0)
    lax.fori_loop(1, n_ens, spread_member, 0)
    wait_sums(0, 8, sum_recv)
    sums[1, z] = jnp.sum(sums[0], axis=0)
    share_sums(1, z, [{"slab": x * 16 + lax.rem(z + at, 8) * 2 + core} for at in range(1, 8)])

    wait_all(recv, recv_sem, 2)
    back = owned(2)
    ball[mine] = back
    share(ball.at[mine], ball.at[mine], 1)

    four = None
    for g in range(4):
        tall = jnp.concatenate([back[:, g * 128 : (g + 1) * 128]] * 16, axis=0)
        part = dot(jnp.where(own, tall, 0.0).astype(BF), tab["from_modes"][g, :128])
        four = part if four is None else four + part
    four = jnp.concatenate([four, four], axis=1)
    tall = jnp.concatenate([(weights_all(g) * four).astype(BF) for g in range(4)], axis=0)
    tall = dot(tall, tab["gather"][...])
    back_modes = jnp.concatenate([fold_all(tall[g * 512 : (g + 1) * 512], own) for g in range(4)], axis=1)
    planes_out(3, back_modes)
    exchange(3)


    wait_sums(1, 8, sum_recv)
    sums[2, mine] = jnp.sum(sums[1], axis=0)
    share_sums(2, mine, [{"ens": lax.rem(mine + at, n_ens)} for at in range(1, n_ens)])
    wait_share(ball, 1)

    def spectral(chunk, carry):
        keep = own_pair(chunk, 128)
        rows = pl.ds(pl.multiple_of(chunk * 128, 128), 128)
        fours = []
        for member in range(n_ens):
            four = to_channels(ball[member], keep)
            fours.append(jnp.concatenate([four, four], axis=1))
        for g in range(4):
            total = None
            for member in range(n_ens):
                part = cexp[member, rows, g * 256 : (g + 1) * 256] * fours[member]
                total = part if total is None else total + part
            gs_v[pl.ds(chunk * 4, 4), :, g * 256 : (g + 1) * 256] = total.reshape(4, 32, 256)
        return carry

    lax.fori_loop(0, 4, spectral, 0)

    wait_all(recv, recv_sem, 3)
    for g in range(4):
        s2[g * 128 : (g + 1) * 128] = narrow(3, g).astype(BF)
    wait_sums(2, n_ens, sum_recv)
    total_out[...] = sums[2, 0] + sums[2, 1] + sums[2, 2] + sums[2, 3]

    for phase in range(4):
        wait_all(send, send_sem, phase)
    for stage, size in enumerate((8, 8, n_ens)):
        wait_sums(stage, size, sum_send)
    wait_share_sent(call, 0)
    wait_share_sent(ball, 1)


def finish_kernel(out_v, gs_v, pre, s2, total, wide, out, gf, gs, gl, gb, gf_v, gl_v, gb_v, sems):
    stores = []
    for part in range(4):
        eight, four = pl.ds(part * 8, 8), pl.ds(part * 4, 4)
        stores.append(pltpu.make_async_copy(gs_v.at[four], gs.at[four], sems.at[part]))
        stores.append(pltpu.make_async_copy(out_v.at[eight], out.at[eight], sems.at[4 + part]))
    for part in range(4):
        gl_v[part * 8 : (part + 1) * 8, :] = total[:8, part * 32 : (part + 1) * 32]
    gb_v[...] = total[8:9, :32]
    stores.append(pltpu.make_async_copy(gl_v, gl, sems.at[24]))
    stores.append(pltpu.make_async_copy(gb_v, gb, sems.at[25]))
    for store in stores:
        store.start()
    for pair in range(4):
        both = dot(s2[...], wide[:, pair * 256 : (pair + 1) * 256])
        for g in range(4):
            some = pl.ds(g * 8 + pair * 2, 2)
            for half in range(2):
                o = g * 8 + pair * 2 + half
                value = both[g * 128 : (g + 1) * 128, half * 128 : (half + 1) * 128]
                gf_v[o] = (value + pre[o]).astype(BF)
            stores.append(pltpu.make_async_copy(gf_v.at[some], gf.at[some], sems.at[8 + pair * 4 + g]))
            stores[-1].start()
    for store in stores:
        store.wait()


def coefs_at(ref, member, g):
    return ref[member, :, g * 128 : (g + 1) * 128]


def wait_all(ref, sem, phase):
    some = ref.at[phase, pl.ds(0, NZ - 1)]
    pltpu.make_async_copy(some, some, sem.at[phase]).wait()


def local(n_slab, n_ens, field, weight, local_weight, bias, cotangent):
    consts = [jnp.asarray(TABLES[name]) for name in NAMES]
    any_spec = pl.BlockSpec(memory_space=pl.ANY)
    vmem = pl.BlockSpec(memory_space=pltpu.VMEM)
    image = (C, N, N)
    dma = pltpu.SemaphoreType.DMA
    held = pl.pallas_call(
        functools.partial(kernel, n_slab, n_ens),
        out_shape=(
            pltpu.VMEM(image, BF),
            pltpu.VMEM((16, 32, 1024), F32),
            pltpu.VMEM(image, F32),
            pltpu.VMEM((512, 256), BF),
            pltpu.VMEM((16, 128), F32),
        ),
        in_specs=[any_spec] * 5 + [any_spec] * len(NAMES),
        out_specs=(vmem,) * 5,
        scratch_shapes=[pltpu.VMEM(TABLES[name].shape, BF) for name in NAMES]
        + [
            pltpu.VMEM(image, BF),
            pltpu.VMEM(image, BF),
            pltpu.VMEM((16, 32, 1024), BF),
            pltpu.VMEM((32, 32), BF),
            pltpu.SMEM((32,), F32),
            pltpu.VMEM(image, BF),
            pltpu.VMEM((512, 512), BF),
            pltpu.VMEM((512, 512), BF),
            pltpu.VMEM((n_ens, 512, 1024), F32),
            pltpu.VMEM((512 + XB, 512), F32),
            pltpu.VMEM((4, NZ, 4, 128), F32),
            pltpu.VMEM((4, NZ, 4, 128), F32),
            pltpu.VMEM((n_ens, K, 512), F32),
            pltpu.VMEM((n_ens, K, 512), F32),
            pltpu.VMEM((3, 8, 16, 128), F32),
            dma((5,)),
            dma((len(NAMES),)),
            dma((4,)),
            dma((4,)),
            dma((2,)),
            dma((2,)),
            dma((3,)),
            dma((3,)),
        ],
        compiler_params=pltpu.CompilerParams(
            collective_id=0, has_side_effects=True, vmem_limit_bytes=57 * 1024 * 1024
        ),
    )(
        field.reshape(image),
        weight,
        local_weight,
        bias,
        cotangent.reshape(image),
        *consts,
    )
    held = [pltpu.with_memory_space_constraint(value, pltpu.VMEM) for value in (*held, jnp.asarray(WIDE))]
    output, grad_field, grad_spectral, grad_local, grad_bias = pl.pallas_call(
        finish_kernel,
        out_shape=(
            jax.ShapeDtypeStruct(image, BF),
            jax.ShapeDtypeStruct(image, BF),
            jax.ShapeDtypeStruct((16, 32, 1024), F32),
            jax.ShapeDtypeStruct((32, 32), F32),
            jax.ShapeDtypeStruct((1, 32), F32),
        ),
        in_specs=[vmem] * 6,
        out_specs=(any_spec,) * 5,
        scratch_shapes=[pltpu.VMEM(image, BF), pltpu.VMEM((32, 32), F32), pltpu.VMEM((1, 32), F32), dma((26,))],
        compiler_params=pltpu.CompilerParams(vmem_limit_bytes=16 * 1024 * 1024),
    )(*held)
    whole = (1, 1) + image
    return (
        output.reshape(whole),
        grad_field.reshape(whole),
        grad_spectral,
        grad_local,
        grad_bias.reshape(32),
    )


def solution(mesh):
    placed = (
        P("ens", "slab", None, None, None),
        P("slab", None, None),
        P(),
        P(),
        P("ens", "slab", None, None, None),
    )
    return jax.shard_map(
        functools.partial(local, mesh.shape["slab"], mesh.shape["ens"]),
        mesh=mesh,
        in_specs=placed,
        out_specs=(
            P("ens", "slab", None, None, None),
            P("ens", "slab", None, None, None),
            P("slab", None, None),
            P(),
            P(),
        ),
        check_vma=False,
    )
```

```python
import functools
import math

import jax
import jax.numpy as jnp
import ml_dtypes
import numpy as np
from jax import lax
from jax.experimental import pallas as pl
from jax.experimental.pallas import tpu as pltpu
from jax.sharding import PartitionSpec as P

BF = jnp.bfloat16
F32 = jnp.float32
MESH = pl.DeviceIdType.MESH
C = 32
N = 128
K = 32
NZ = 64
XB = 16
ROOT = math.sqrt(2.0 / math.pi)


def basis_table(modes, length):
    frequency = np.arange(modes, dtype=np.int32) - modes // 2
    points = np.arange(length, dtype=np.int32)
    product = frequency[:, None] * points[None, :] % length
    angles = product.astype(np.float32) * np.float32(2.0 * math.pi / length)
    return (np.cos(angles) + np.sin(angles)) / np.float32(math.sqrt(length))


def split_table(table):
    high = table.astype(ml_dtypes.bfloat16)
    low = (table - high.astype(np.float32)).astype(ml_dtypes.bfloat16)
    return high, low


def three(table):
    high, low = split_table(table)
    return np.concatenate([high, high, low], axis=1)


def tables():
    basis = basis_table(K, N)
    slots = np.arange(NZ)
    basis_z = basis_table(K, NZ)[:, slots % 32 * 2 + slots // 32]

    def widen(table):
        wide = np.zeros((2, 8, 16, 8, N), np.float32)
        for c in range(8):
            wide[:, c, :, c, :] = table.astype(np.float32).reshape(2, 16, N)
        return wide.reshape(256, 8 * N)

    high, low = (widen(table) for table in split_table(basis))
    eye8, eye32 = np.eye(8, dtype=np.float32), np.eye(32, dtype=np.float32)
    spread = np.repeat(np.repeat(eye8, 16, axis=0), 32, axis=1)
    to_modes = np.tile(np.repeat(eye32, 16, axis=1), (4, 1))
    from_modes = to_modes.T.reshape(4, 128, 128)
    rows = np.repeat(eye32, XB, axis=0)
    lanes = np.tile(rows, (1, 4))
    return dict(
        wide_t=high.T.copy(),
        bx=three(basis),
        wide=np.concatenate([high, high, low], axis=0),
        bz=three(basis_z),
        spread=np.concatenate([spread, spread], axis=0),
        to_modes=np.concatenate([to_modes, to_modes], axis=0),
        bzt=three(basis_z.T),
        bxt=three(basis.T),
        rows=rows,
        rows_t=rows.T.copy(),
        lanes=lanes,
        from_modes=np.concatenate([from_modes, from_modes], axis=1),
        gather=spread.T.copy(),
    )


TABLES = {name: np.asarray(table).astype(ml_dtypes.bfloat16) for name, table in tables().items()}
NAMES = tuple(TABLES)
WIDE = TABLES["wide"][:256]


def split(value):
    high = value.astype(BF)
    return high, (value - high.astype(F32)).astype(BF)


def dot(a, b):
    return jnp.dot(a, b, preferred_element_type=F32)


def dot_nt(a, b):
    return lax.dot_general(a, b, (((1,), (1,)), ((), ())), preferred_element_type=F32)


def dot_three(table, value):
    high, low = split(value)
    return dot(table, jnp.concatenate([high, low, high], axis=0))


def middle_out(at, size):
    return size // 2 + (at + 1) // 2 * (2 * lax.rem(at + 1, 2) - 1)


def kernel(n_slab, n_ens, field, weight, lw_in, bias_in, cot, *rest):
    consts = dict(zip(NAMES, rest[: len(NAMES)]))
    rest = rest[len(NAMES) :]
    out_v, gs_v, pre, s2, total_out = rest[:5]
    rest = rest[5:]
    tab = dict(zip(NAMES, rest[: len(NAMES)]))
    rest = rest[len(NAMES) :]
    (
        field_v, cot_v, w_v, lw, bias, slope_v, kl_f, kl_b, cexp, gacc,
        send, recv, call, ball, sums,
        load_sem, tab_sem, send_sem, recv_sem, ens_send, ens_recv, sum_send, sum_recv,
    ) = rest
    me = lax.axis_index("slab")
    mine = lax.axis_index("ens")
    x, z, core = me // 16, lax.rem(me // 2, 8), lax.rem(me, 2)
    my_slot = core * 32 + me // 2
    places = [(lax.rem(x + at, 4), lax.rem(core + 1 + other, 2)) for at in (2, 1, 3, 0) for other in range(2)]

    barrier = pltpu.get_barrier_semaphore()

    def greet(at, carry):
        pl.semaphore_signal(barrier, inc=1, device_id={"slab": lax.rem(me + at, n_slab)}, device_id_type=MESH)
        return carry

    lax.fori_loop(1, n_slab, greet, 0, unroll=21)
    for at in range(1, n_ens):
        pl.semaphore_signal(barrier, inc=1, device_id={"ens": lax.rem(mine + at, n_ens)}, device_id_type=MESH)

    loads = [
        pltpu.make_async_copy(field, field_v, load_sem.at[0]),
        pltpu.make_async_copy(cot, cot_v, load_sem.at[1]),
        pltpu.make_async_copy(weight, w_v, load_sem.at[2]),
        pltpu.make_async_copy(lw_in, lw, load_sem.at[3]),
        pltpu.make_async_copy(bias_in, bias, load_sem.at[4]),
    ]
    tab_loads = {
        name: pltpu.make_async_copy(consts[name], tab[name], tab_sem.at[at])
        for at, name in enumerate(NAMES)
    }
    tab_loads["wide_t"].start()
    loads[0].start()
    for name in NAMES[1:]:
        tab_loads[name].start()
    for load in loads[1:]:
        load.start()

    def project(data, pair):
        tall = jnp.concatenate([jnp.concatenate(both, axis=1) for both in data], axis=0)
        return dot(tall, tab["wide_t"][pair * 256 : (pair + 1) * 256, :])

    def exchange(phase):
        def one(to_x, to_z, to_core):
            pltpu.make_async_remote_copy(
                src_ref=send.at[phase, to_core * 32 + to_x * 8 + to_z],
                dst_ref=recv.at[phase, my_slot],
                send_sem=send_sem.at[phase],
                recv_sem=recv_sem.at[phase],
                device_id={"slab": to_x * 16 + to_z * 2 + to_core},
                device_id_type=MESH,
            ).start()

        def ring(at, carry):
            to_z = lax.rem(z + middle_out(at, 8), 8)
            for to_x, to_core in places:
                one(to_x, to_z, to_core)
            return carry

        def both(at, carry):
            for to in (4 - at, 4 + at):
                to_z = lax.rem(z + to, 8)
                for to_x, to_core in places:
                    one(to_x, to_z, to_core)
            return carry

        for to_x, to_core in places:
            one(to_x, lax.rem(z + 4, 8), to_core)
        lax.fori_loop(1, 4, both, 0)
        for to_x, to_core in places[:-1]:
            one(to_x, z, to_core)
        recv[phase, my_slot] = send[phase, my_slot]

    def share(source, target, at_sem):
        for at in range(1, n_ens):
            pltpu.make_async_remote_copy(
                src_ref=source,
                dst_ref=target,
                send_sem=ens_send.at[at_sem],
                recv_sem=ens_recv.at[at_sem],
                device_id={"ens": lax.rem(mine + at, n_ens)},
                device_id_type=MESH,
            ).start()

    def wait_share(ref, at_sem):
        some = ref.at[pl.ds(0, n_ens - 1)]
        pltpu.make_async_copy(some, some, ens_recv.at[at_sem]).wait()

    def wait_share_sent(ref, at_sem):
        some = ref.at[pl.ds(0, n_ens - 1)]
        pltpu.make_async_copy(some, some, ens_send.at[at_sem]).wait()

    def share_sums(stage, place, peers):
        for peer in peers:
            pltpu.make_async_remote_copy(
                src_ref=sums.at[stage, place],
                dst_ref=sums.at[stage, place],
                send_sem=sum_send.at[stage],
                recv_sem=sum_recv.at[stage],
                device_id=peer,
                device_id_type=MESH,
            ).start()

    def wait_sums(stage, size, sem):
        some = sums.at[stage, pl.ds(0, size - 1)]
        pltpu.make_async_copy(some, some, sem.at[stage]).wait()

    def owned(phase):
        planes = jnp.concatenate([recv[phase, :, g, :] for g in range(4)], axis=1)
        return dot_three(tab["bz"][...], planes)

    def planes_out(phase, modes):
        planes = dot_three(tab["bzt"][...], modes)
        for g in range(4):
            send[phase, :, g, :] = planes[:, g * 128 : (g + 1) * 128]

    def own_pair(chunk, lanes):
        row = lax.broadcasted_iota(jnp.int32, (128, lanes), 0) // 32 + chunk * 4
        lane = lax.rem(lax.broadcasted_iota(jnp.int32, (128, lanes), 1), 16)
        return row == lane

    def masked(modes, keep):
        tall = jnp.concatenate([modes] * 4, axis=0)
        high, low = split(jnp.where(keep, tall, 0.0))
        return jnp.concatenate([high, low], axis=1)

    def to_channels(modes, keep):
        total = None
        for g in range(4):
            part = dot(masked(modes[:, g * 128 : (g + 1) * 128], keep), tab["from_modes"][g])
            total = part if total is None else total + part
        return total

    def own_pair_all(lanes):
        row = lax.broadcasted_iota(jnp.int32, (512, lanes), 0) // 32
        return row == lax.rem(lax.broadcasted_iota(jnp.int32, (512, lanes), 1), 16)

    def fold_all(value, keep):
        return jnp.sum(jnp.where(keep, value, 0.0).reshape(16, 32, value.shape[1]), axis=0)

    def weights_all(g):
        return w_v[:, :, g * 256 : (g + 1) * 256].reshape(512, 256).astype(F32)

    def narrow(phase, g):
        modes = jnp.concatenate([recv[phase, :32, g, :], recv[phase, 32:, g, :]], axis=1)
        return dot_three(tab["bxt"][...], modes)

    def put(phase, total):
        for g in range(4):
            modes = dot_three(tab["bx"][...], total[g * 128 : (g + 1) * 128])
            send[phase, :32, g, :] = modes[:, :128]
            send[phase, 32:, g, :] = modes[:, 128:]

    def block_of(ref, at):
        a = ref[:, pl.ds(pl.multiple_of(at * 2 * XB, 2 * XB), XB), :].reshape(C * XB, N)
        b = ref[:, pl.ds(pl.multiple_of(at * 2 * XB + XB, XB), XB), :].reshape(C * XB, N)
        return jnp.concatenate([a, b], axis=1)

    def pointwise(matrix, data):
        def step(at, carry):
            value = dot(matrix[...], block_of(data, at))
            pre[:, pl.ds(pl.multiple_of(at * 2 * XB, 2 * XB), XB), :] = value[:, :N].reshape(C, XB, N)
            pre[:, pl.ds(pl.multiple_of(at * 2 * XB + XB, XB), XB), :] = value[:, N:].reshape(C, XB, N)
            return carry

        lax.fori_loop(0, N // (2 * XB), step, 0)

    tab_loads["wide_t"].wait()
    tab_loads["bx"].wait()
    loads[0].wait()
    total = None
    for pair in range(4):
        part = project([[field_v[g * 8 + pair * 2 + half] for half in range(2)] for g in range(4)], pair)
        total = part if total is None else total + part
    put(0, total)
    pl.semaphore_wait(barrier, n_slab - 1 + n_ens - 1)
    exchange(0)

    for name in NAMES[2:]:
        tab_loads[name].wait()
    for load in loads[1:]:
        load.wait()
    tall = dot(dot_nt(tab["rows"][...], lw[...]).astype(BF), tab["rows_t"][...])
    same = lax.rem(lax.broadcasted_iota(jnp.int32, (512, 512), 0), XB) == lax.rem(
        lax.broadcasted_iota(jnp.int32, (512, 512), 1), XB
    )
    kl_f[...] = jnp.where(same, tall, 0.0).astype(BF)
    tall = dot(dot(tab["rows"][...], lw[...]).astype(BF), tab["rows_t"][...])
    kl_b[...] = jnp.where(same, tall, 0.0).astype(BF)
    pointwise(kl_f, field_v)

    def add_bias(o, carry):
        pre[o] = pre[o] + bias[o]
        return carry

    lax.fori_loop(0, C, add_bias, 0)

    wait_all(recv, recv_sem, 0)
    coefs = owned(0)
    call[mine] = coefs

    own, own_wide = own_pair_all(128), own_pair_all(512)
    part = None
    for g in range(4):
        high, low = split(jnp.where(own, jnp.concatenate([coefs[:, g * 128 : (g + 1) * 128]] * 16, axis=0), 0.0))
        value = dot(jnp.concatenate([high, low], axis=1), tab["spread"][...]) * weights_all(g)
        value = value[:, :128] + value[:, 128:]
        part = value if part is None else part + value
    high, low = split(part)
    mixed = fold_all(dot(jnp.concatenate([high, low], axis=1), tab["to_modes"][...]), own_wide)
    planes_out(1, mixed)
    exchange(1)


    def spread_member(at, carry):
        member = lax.rem(mine + at, n_ens)
        for chunk in range(4):
            keep = own_pair(chunk, 128)
            for g in range(4):
                cexp[member, chunk * 128 : (chunk + 1) * 128, g * 256 : (g + 1) * 256] = dot(
                    masked(coefs_at(call, member, g), keep), tab["spread"][...]
                )
        return carry

    spread_member(0, 0)

    wait_all(recv, recv_sem, 1)
    share(call.at[mine], call.at[mine], 0)
    narrowed = []
    for g in range(4):
        high, low = split(narrow(1, g))
        narrowed.append(jnp.concatenate([high, low, high], axis=1))
    narrowed = jnp.concatenate(narrowed, axis=0)
    total = None
    for pair in range(4):
        both = dot(narrowed, tab["wide"][:, pair * 256 : (pair + 1) * 256])
        slopes = []
        for g in range(4):
            slopes.append([])
            for half in range(2):
                o = g * 8 + pair * 2 + half
                v = both[g * 128 : (g + 1) * 128, half * 128 : (half + 1) * 128] + pre[o]
                cubic = (ROOT * 0.044715) * (v * v)
                t = jnp.tanh(v * (ROOT + cubic))
                h = 0.5 * v
                more = 1.0 + t
                out_v[o] = (h * more).astype(BF)
                grad = more * (0.5 + (h * (ROOT + 3.0 * cubic)) * (1.0 - t))
                slope = (cot_v[o].astype(F32) * grad).astype(BF)
                slope_v[o] = slope
                slopes[g].append(slope)
        part = project(slopes, pair)
        total = part if total is None else total + part
    put(2, total)

    exchange(2)

    gacc[...] = jnp.zeros_like(gacc)

    def outer(at, carry):
        ones = jnp.ones((XB, 2 * N), BF)
        gacc[...] += dot_nt(jnp.concatenate([block_of(field_v, at), ones], axis=0), block_of(slope_v, at))
        return carry

    lax.fori_loop(0, N // (2 * XB), outer, 0)
    same = lax.rem(lax.broadcasted_iota(jnp.int32, (512, 512), 0), XB) == lax.rem(
        lax.broadcasted_iota(jnp.int32, (512, 512), 1), XB
    )
    rows = jnp.sum(jnp.where(same, gacc[: C * XB], 0.0).reshape(C, XB, 512), axis=1)
    bias_rows = gacc[C * XB : C * XB + XB]
    high, low = split(jnp.concatenate([rows, bias_rows], axis=0))
    rows = dot(high, tab["lanes"][...]) + dot(low, tab["lanes"][...])
    lane = lax.broadcasted_iota(jnp.int32, (8, 128), 1) // 32
    packed = jnp.zeros((8, 128), F32)
    for part in range(4):
        packed = packed + jnp.where(lane == part, rows[part * 8 : (part + 1) * 8], 0.0)
    near = x * 2 + core
    sums[0, near, :8] = packed
    sums[0, near, 8:] = rows[C : C + 8]
    peers = [lax.rem(near + at, 8) for at in range(1, 8)]
    share_sums(0, near, [{"slab": peer // 2 * 16 + z * 2 + lax.rem(peer, 2)} for peer in peers])
    pointwise(kl_b, slope_v)
    wait_share(call, 0)
    lax.fori_loop(1, n_ens, spread_member, 0)
    wait_sums(0, 8, sum_recv)
    sums[1, z] = jnp.sum(sums[0], axis=0)
    share_sums(1, z, [{"slab": x * 16 + lax.rem(z + at, 8) * 2 + core} for at in range(1, 8)])

    wait_all(recv, recv_sem, 2)
    back = owned(2)
    ball[mine] = back
    share(ball.at[mine], ball.at[mine], 1)

    four = None
    for g in range(4):
        tall = jnp.concatenate([back[:, g * 128 : (g + 1) * 128]] * 16, axis=0)
        part = dot(jnp.where(own, tall, 0.0).astype(BF), tab["from_modes"][g, :128])
        four = part if four is None else four + part
    four = jnp.concatenate([four, four], axis=1)
    tall = jnp.concatenate([(weights_all(g) * four).astype(BF) for g in range(4)], axis=0)
    tall = dot(tall, tab["gather"][...])
    back_modes = jnp.concatenate([fold_all(tall[g * 512 : (g + 1) * 512], own) for g in range(4)], axis=1)
    planes_out(3, back_modes)
    exchange(3)


    wait_sums(1, 8, sum_recv)
    sums[2, mine] = jnp.sum(sums[1], axis=0)
    share_sums(2, mine, [{"ens": lax.rem(mine + at, n_ens)} for at in range(1, n_ens)])
    wait_share(ball, 1)

    def spectral(chunk, carry):
        keep = own_pair(chunk, 128)
        rows = pl.ds(pl.multiple_of(chunk * 128, 128), 128)
        fours = []
        for member in range(n_ens):
            four = to_channels(ball[member], keep)
            fours.append(jnp.concatenate([four, four], axis=1))
        for g in range(4):
            total = None
            for member in range(n_ens):
                part = cexp[member, rows, g * 256 : (g + 1) * 256] * fours[member]
                total = part if total is None else total + part
            gs_v[pl.ds(chunk * 4, 4), :, g * 256 : (g + 1) * 256] = total.reshape(4, 32, 256)
        return carry

    lax.fori_loop(0, 4, spectral, 0)

    wait_all(recv, recv_sem, 3)
    for g in range(4):
        s2[g * 128 : (g + 1) * 128] = narrow(3, g).astype(BF)
    wait_sums(2, n_ens, sum_recv)
    total_out[...] = sums[2, 0] + sums[2, 1] + sums[2, 2] + sums[2, 3]

    for phase in range(4):
        wait_all(send, send_sem, phase)
    for stage, size in enumerate((8, 8, n_ens)):
        wait_sums(stage, size, sum_send)
    wait_share_sent(call, 0)
    wait_share_sent(ball, 1)


def finish_kernel(out_v, gs_v, pre, s2, total, wide, out, gf, gs, gl, gb, gf_v, gl_v, gb_v, sems):
    stores = []
    for part in range(4):
        eight, four = pl.ds(part * 8, 8), pl.ds(part * 4, 4)
        stores.append(pltpu.make_async_copy(gs_v.at[four], gs.at[four], sems.at[part]))
        stores.append(pltpu.make_async_copy(out_v.at[eight], out.at[eight], sems.at[4 + part]))
    for part in range(4):
        gl_v[part * 8 : (part + 1) * 8, :] = total[:8, part * 32 : (part + 1) * 32]
    gb_v[...] = total[8:9, :32]
    stores.append(pltpu.make_async_copy(gl_v, gl, sems.at[24]))
    stores.append(pltpu.make_async_copy(gb_v, gb, sems.at[25]))
    for store in stores:
        store.start()
    for pair in range(4):
        both = dot(s2[...], wide[:, pair * 256 : (pair + 1) * 256])
        for g in range(4):
            some = pl.ds(g * 8 + pair * 2, 2)
            for half in range(2):
                o = g * 8 + pair * 2 + half
                value = both[g * 128 : (g + 1) * 128, half * 128 : (half + 1) * 128]
                gf_v[o] = (value + pre[o]).astype(BF)
            stores.append(pltpu.make_async_copy(gf_v.at[some], gf.at[some], sems.at[8 + pair * 4 + g]))
            stores[-1].start()
    for store in stores:
        store.wait()


def coefs_at(ref, member, g):
    return ref[member, :, g * 128 : (g + 1) * 128]


def wait_all(ref, sem, phase):
    some = ref.at[phase, pl.ds(0, NZ - 1)]
    pltpu.make_async_copy(some, some, sem.at[phase]).wait()


def local(n_slab, n_ens, field, weight, local_weight, bias, cotangent):
    consts = [jnp.asarray(TABLES[name]) for name in NAMES]
    any_spec = pl.BlockSpec(memory_space=pl.ANY)
    vmem = pl.BlockSpec(memory_space=pltpu.VMEM)
    image = (C, N, N)
    dma = pltpu.SemaphoreType.DMA
    held = pl.pallas_call(
        functools.partial(kernel, n_slab, n_ens),
        out_shape=(
            pltpu.VMEM(image, BF),
            pltpu.VMEM((16, 32, 1024), F32),
            pltpu.VMEM(image, F32),
            pltpu.VMEM((512, 256), BF),
            pltpu.VMEM((16, 128), F32),
        ),
        in_specs=[any_spec] * 5 + [any_spec] * len(NAMES),
        out_specs=(vmem,) * 5,
        scratch_shapes=[pltpu.VMEM(TABLES[name].shape, BF) for name in NAMES]
        + [
            pltpu.VMEM(image, BF),
            pltpu.VMEM(image, BF),
            pltpu.VMEM((16, 32, 1024), BF),
            pltpu.VMEM((32, 32), BF),
            pltpu.SMEM((32,), F32),
            pltpu.VMEM(image, BF),
            pltpu.VMEM((512, 512), BF),
            pltpu.VMEM((512, 512), BF),
            pltpu.VMEM((n_ens, 512, 1024), F32),
            pltpu.VMEM((512 + XB, 512), F32),
            pltpu.VMEM((4, NZ, 4, 128), F32),
            pltpu.VMEM((4, NZ, 4, 128), F32),
            pltpu.VMEM((n_ens, K, 512), F32),
            pltpu.VMEM((n_ens, K, 512), F32),
            pltpu.VMEM((3, 8, 16, 128), F32),
            dma((5,)),
            dma((len(NAMES),)),
            dma((4,)),
            dma((4,)),
            dma((2,)),
            dma((2,)),
            dma((3,)),
            dma((3,)),
        ],
        compiler_params=pltpu.CompilerParams(
            collective_id=0, has_side_effects=True, vmem_limit_bytes=57 * 1024 * 1024
        ),
    )(
        field.reshape(image),
        weight,
        local_weight,
        bias,
        cotangent.reshape(image),
        *consts,
    )
    held = [pltpu.with_memory_space_constraint(value, pltpu.VMEM) for value in (*held, jnp.asarray(WIDE))]
    output, grad_field, grad_spectral, grad_local, grad_bias = pl.pallas_call(
        finish_kernel,
        out_shape=(
            jax.ShapeDtypeStruct(image, BF),
            jax.ShapeDtypeStruct(image, BF),
            jax.ShapeDtypeStruct((16, 32, 1024), F32),
            jax.ShapeDtypeStruct((32, 32), F32),
            jax.ShapeDtypeStruct((1, 32), F32),
        ),
        in_specs=[vmem] * 6,
        out_specs=(any_spec,) * 5,
        scratch_shapes=[pltpu.VMEM(image, BF), pltpu.VMEM((32, 32), F32), pltpu.VMEM((1, 32), F32), dma((26,))],
        compiler_params=pltpu.CompilerParams(vmem_limit_bytes=16 * 1024 * 1024),
    )(*held)
    whole = (1, 1) + image
    return (
        output.reshape(whole),
        grad_field.reshape(whole),
        grad_spectral,
        grad_local,
        grad_bias.reshape(32),
    )


def solution(mesh):
    placed = (
        P("ens", "slab", None, None, None),
        P("slab", None, None),
        P(),
        P(),
        P("ens", "slab", None, None, None),
    )
    return jax.shard_map(
        functools.partial(local, mesh.shape["slab"], mesh.shape["ens"]),
        mesh=mesh,
        in_specs=placed,
        out_specs=(
            P("ens", "slab", None, None, None),
            P("ens", "slab", None, None, None),
            P("slab", None, None),
            P(),
            P(),
        ),
        check_vma=False,
    )
```

```python
import functools
import math

import jax
import jax.numpy as jnp
import ml_dtypes
import numpy as np
from jax import lax
from jax.experimental import pallas as pl
from jax.experimental.pallas import tpu as pltpu
from jax.sharding import PartitionSpec as P

BF = jnp.bfloat16
F32 = jnp.float32
MESH = pl.DeviceIdType.MESH
C = 32
N = 128
K = 32
NZ = 64
XB = 16
ROOT = math.sqrt(2.0 / math.pi)


def basis_table(modes, length):
    frequency = np.arange(modes, dtype=np.int32) - modes // 2
    points = np.arange(length, dtype=np.int32)
    product = frequency[:, None] * points[None, :] % length
    angles = product.astype(np.float32) * np.float32(2.0 * math.pi / length)
    return (np.cos(angles) + np.sin(angles)) / np.float32(math.sqrt(length))


def split_table(table):
    high = table.astype(ml_dtypes.bfloat16)
    low = (table - high.astype(np.float32)).astype(ml_dtypes.bfloat16)
    return high, low


def three(table):
    high, low = split_table(table)
    return np.concatenate([high, high, low], axis=1)


def tables():
    basis = basis_table(K, N)
    slots = np.arange(NZ)
    basis_z = basis_table(K, NZ)[:, slots % 32 * 2 + slots // 32]

    def widen(table):
        wide = np.zeros((2, 8, 16, 8, N), np.float32)
        for c in range(8):
            wide[:, c, :, c, :] = table.astype(np.float32).reshape(2, 16, N)
        return wide.reshape(256, 8 * N)

    high, low = (widen(table) for table in split_table(basis))
    eye8, eye32 = np.eye(8, dtype=np.float32), np.eye(32, dtype=np.float32)
    spread = np.repeat(np.repeat(eye8, 16, axis=0), 32, axis=1)
    to_modes = np.tile(np.repeat(eye32, 16, axis=1), (4, 1))
    from_modes = to_modes.T.reshape(4, 128, 128)
    rows = np.repeat(eye32, XB, axis=0)
    lanes = np.tile(rows, (1, 4))
    return dict(
        wide_t=high.T.copy(),
        bx=three(basis),
        wide=np.concatenate([high, high, low], axis=0),
        bz=three(basis_z),
        spread=np.concatenate([spread, spread], axis=0),
        to_modes=np.concatenate([to_modes, to_modes], axis=0),
        bzt=three(basis_z.T),
        bxt=three(basis.T),
        rows=rows,
        rows_t=rows.T.copy(),
        lanes=lanes,
        from_modes=np.concatenate([from_modes, from_modes], axis=1),
        gather=spread.T.copy(),
    )


TABLES = {name: np.asarray(table).astype(ml_dtypes.bfloat16) for name, table in tables().items()}
NAMES = tuple(TABLES)
WIDE = TABLES["wide"][:256]


def split(value):
    high = value.astype(BF)
    return high, (value - high.astype(F32)).astype(BF)


def dot(a, b):
    return jnp.dot(a, b, preferred_element_type=F32)


def dot_nt(a, b):
    return lax.dot_general(a, b, (((1,), (1,)), ((), ())), preferred_element_type=F32)


def dot_three(table, value):
    high, low = split(value)
    return dot(table, jnp.concatenate([high, low, high], axis=0))


def middle_out(at, size):
    return size // 2 + (at + 1) // 2 * (2 * lax.rem(at + 1, 2) - 1)


def kernel(n_slab, n_ens, field, weight, lw_in, bias_in, cot, *rest):
    consts = dict(zip(NAMES, rest[: len(NAMES)]))
    rest = rest[len(NAMES) :]
    out_v, gs_v, pre, s2, total_out = rest[:5]
    rest = rest[5:]
    tab = dict(zip(NAMES, rest[: len(NAMES)]))
    rest = rest[len(NAMES) :]
    (
        field_v, cot_v, w_v, lw, bias, slope_v, kl_f, kl_b, cexp, gacc,
        send, recv, call, ball, sums,
        load_sem, tab_sem, send_sem, recv_sem, ens_send, ens_recv, sum_send, sum_recv,
    ) = rest
    me = lax.axis_index("slab")
    mine = lax.axis_index("ens")
    x, z, core = me // 16, lax.rem(me // 2, 8), lax.rem(me, 2)
    my_slot = core * 32 + me // 2
    places = [(lax.rem(x + at, 4), lax.rem(core + 1 + other, 2)) for at in (2, 1, 3, 0) for other in range(2)]

    barrier = pltpu.get_barrier_semaphore()

    def greet(at, carry):
        pl.semaphore_signal(barrier, inc=1, device_id={"slab": lax.rem(me + at, n_slab)}, device_id_type=MESH)
        return carry

    lax.fori_loop(1, n_slab, greet, 0, unroll=21)
    for at in range(1, n_ens):
        pl.semaphore_signal(barrier, inc=1, device_id={"ens": lax.rem(mine + at, n_ens)}, device_id_type=MESH)

    loads = [
        pltpu.make_async_copy(field, field_v, load_sem.at[0]),
        pltpu.make_async_copy(cot, cot_v, load_sem.at[1]),
        pltpu.make_async_copy(weight, w_v, load_sem.at[2]),
        pltpu.make_async_copy(lw_in, lw, load_sem.at[3]),
        pltpu.make_async_copy(bias_in, bias, load_sem.at[4]),
    ]
    tab_loads = {
        name: pltpu.make_async_copy(consts[name], tab[name], tab_sem.at[at])
        for at, name in enumerate(NAMES)
    }
    tab_loads["wide_t"].start()
    loads[0].start()
    for name in NAMES[1:]:
        tab_loads[name].start()
    for load in loads[1:]:
        load.start()

    def project(data, pair):
        tall = jnp.concatenate([jnp.concatenate(both, axis=1) for both in data], axis=0)
        return dot(tall, tab["wide_t"][pair * 256 : (pair + 1) * 256, :])

    def exchange(phase):
        def one(to_x, to_z, to_core):
            pltpu.make_async_remote_copy(
                src_ref=send.at[phase, to_core * 32 + to_x * 8 + to_z],
                dst_ref=recv.at[phase, my_slot],
                send_sem=send_sem.at[phase],
                recv_sem=recv_sem.at[phase],
                device_id={"slab": to_x * 16 + to_z * 2 + to_core},
                device_id_type=MESH,
            ).start()

        def ring(at, carry):
            to_z = lax.rem(z + middle_out(at, 8), 8)
            for to_x, to_core in places:
                one(to_x, to_z, to_core)
            return carry

        def both(at, carry):
            for to in (4 - at, 4 + at):
                to_z = lax.rem(z + to, 8)
                for to_x, to_core in places:
                    one(to_x, to_z, to_core)
            return carry

        for to_x, to_core in places:
            one(to_x, lax.rem(z + 4, 8), to_core)
        lax.fori_loop(1, 4, both, 0)
        for to_x, to_core in places[:-1]:
            one(to_x, z, to_core)
        recv[phase, my_slot] = send[phase, my_slot]

    def share(source, target, at_sem):
        for at in range(1, n_ens):
            pltpu.make_async_remote_copy(
                src_ref=source,
                dst_ref=target,
                send_sem=ens_send.at[at_sem],
                recv_sem=ens_recv.at[at_sem],
                device_id={"ens": lax.rem(mine + at, n_ens)},
                device_id_type=MESH,
            ).start()

    def wait_share(ref, at_sem):
        some = ref.at[pl.ds(0, n_ens - 1)]
        pltpu.make_async_copy(some, some, ens_recv.at[at_sem]).wait()

    def wait_share_sent(ref, at_sem):
        some = ref.at[pl.ds(0, n_ens - 1)]
        pltpu.make_async_copy(some, some, ens_send.at[at_sem]).wait()

    def share_sums(stage, place, peers):
        for peer in peers:
            pltpu.make_async_remote_copy(
                src_ref=sums.at[stage, place],
                dst_ref=sums.at[stage, place],
                send_sem=sum_send.at[stage],
                recv_sem=sum_recv.at[stage],
                device_id=peer,
                device_id_type=MESH,
            ).start()

    def wait_sums(stage, size, sem):
        some = sums.at[stage, pl.ds(0, size - 1)]
        pltpu.make_async_copy(some, some, sem.at[stage]).wait()

    def owned(phase):
        planes = jnp.concatenate([recv[phase, :, g, :] for g in range(4)], axis=1)
        return dot_three(tab["bz"][...], planes)

    def planes_out(phase, modes):
        planes = dot_three(tab["bzt"][...], modes)
        for g in range(4):
            send[phase, :, g, :] = planes[:, g * 128 : (g + 1) * 128]

    def own_pair(chunk, lanes):
        row = lax.broadcasted_iota(jnp.int32, (128, lanes), 0) // 32 + chunk * 4
        lane = lax.rem(lax.broadcasted_iota(jnp.int32, (128, lanes), 1), 16)
        return row == lane

    def masked(modes, keep):
        tall = jnp.concatenate([modes] * 4, axis=0)
        high, low = split(jnp.where(keep, tall, 0.0))
        return jnp.concatenate([high, low], axis=1)

    def to_channels(modes, keep):
        total = None
        for g in range(4):
            part = dot(masked(modes[:, g * 128 : (g + 1) * 128], keep), tab["from_modes"][g])
            total = part if total is None else total + part
        return total

    def own_pair_all(lanes):
        lane = lax.rem(lax.broadcasted_iota(jnp.int32, (32, lanes), 1), 16)
        row = jnp.concatenate([jnp.full((32, lanes), j, jnp.int32) for j in range(16)], axis=0)
        return row == jnp.concatenate([lane] * 16, axis=0)

    def fold_all(value, keep):
        return jnp.sum(jnp.where(keep, value, 0.0).reshape(16, 32, value.shape[1]), axis=0)

    def weights_all(g):
        return w_v[:, :, g * 256 : (g + 1) * 256].reshape(512, 256).astype(F32)

    def narrow(phase, g):
        modes = jnp.concatenate([recv[phase, :32, g, :], recv[phase, 32:, g, :]], axis=1)
        return dot_three(tab["bxt"][...], modes)

    def put(phase, total):
        for g in range(4):
            modes = dot_three(tab["bx"][...], total[g * 128 : (g + 1) * 128])
            send[phase, :32, g, :] = modes[:, :128]
            send[phase, 32:, g, :] = modes[:, 128:]

    def block_of(ref, at):
        a = ref[:, pl.ds(pl.multiple_of(at * 2 * XB, 2 * XB), XB), :].reshape(C * XB, N)
        b = ref[:, pl.ds(pl.multiple_of(at * 2 * XB + XB, XB), XB), :].reshape(C * XB, N)
        return jnp.concatenate([a, b], axis=1)

    def pointwise(matrix, data):
        def step(at, carry):
            value = dot(matrix[...], block_of(data, at))
            pre[:, pl.ds(pl.multiple_of(at * 2 * XB, 2 * XB), XB), :] = value[:, :N].reshape(C, XB, N)
            pre[:, pl.ds(pl.multiple_of(at * 2 * XB + XB, XB), XB), :] = value[:, N:].reshape(C, XB, N)
            return carry

        lax.fori_loop(0, N // (2 * XB), step, 0)

    tab_loads["wide_t"].wait()
    tab_loads["bx"].wait()
    loads[0].wait()
    total = None
    for pair in range(4):
        part = project([[field_v[g * 8 + pair * 2 + half] for half in range(2)] for g in range(4)], pair)
        total = part if total is None else total + part
    put(0, total)
    pl.semaphore_wait(barrier, n_slab - 1 + n_ens - 1)
    exchange(0)

    for name in NAMES[2:]:
        tab_loads[name].wait()
    for load in loads[1:]:
        load.wait()
    tall = dot(dot_nt(tab["rows"][...], lw[...]).astype(BF), tab["rows_t"][...])
    same = lax.rem(lax.broadcasted_iota(jnp.int32, (512, 512), 0), XB) == lax.rem(
        lax.broadcasted_iota(jnp.int32, (512, 512), 1), XB
    )
    kl_f[...] = jnp.where(same, tall, 0.0).astype(BF)
    tall = dot(dot(tab["rows"][...], lw[...]).astype(BF), tab["rows_t"][...])
    kl_b[...] = jnp.where(same, tall, 0.0).astype(BF)
    pointwise(kl_f, field_v)

    def add_bias(o, carry):
        pre[o] = pre[o] + bias[o]
        return carry

    lax.fori_loop(0, C, add_bias, 0)

    wait_all(recv, recv_sem, 0)
    coefs = owned(0)
    call[mine] = coefs

    own, own_wide = own_pair_all(128), own_pair_all(512)
    part = None
    for g in range(4):
        high, low = split(jnp.where(own, jnp.concatenate([coefs[:, g * 128 : (g + 1) * 128]] * 16, axis=0), 0.0))
        value = dot(jnp.concatenate([high, low], axis=1), tab["spread"][...]) * weights_all(g)
        value = value[:, :128] + value[:, 128:]
        part = value if part is None else part + value
    high, low = split(part)
    mixed = fold_all(dot(jnp.concatenate([high, low], axis=1), tab["to_modes"][...]), own_wide)
    planes_out(1, mixed)
    exchange(1)


    def spread_member(at, carry):
        member = lax.rem(mine + at, n_ens)
        for chunk in range(4):
            keep = own_pair(chunk, 128)
            for g in range(4):
                cexp[member, chunk * 128 : (chunk + 1) * 128, g * 256 : (g + 1) * 256] = dot(
                    masked(coefs_at(call, member, g), keep), tab["spread"][...]
                )
        return carry

    spread_member(0, 0)

    wait_all(recv, recv_sem, 1)
    share(call.at[mine], call.at[mine], 0)
    narrowed = []
    for g in range(4):
        high, low = split(narrow(1, g))
        narrowed.append(jnp.concatenate([high, low, high], axis=1))
    narrowed = jnp.concatenate(narrowed, axis=0)
    total = None
    for pair in range(4):
        both = dot(narrowed, tab["wide"][:, pair * 256 : (pair + 1) * 256])
        slopes = []
        for g in range(4):
            slopes.append([])
            for half in range(2):
                o = g * 8 + pair * 2 + half
                v = both[g * 128 : (g + 1) * 128, half * 128 : (half + 1) * 128] + pre[o]
                cubic = (ROOT * 0.044715) * (v * v)
                t = jnp.tanh(v * (ROOT + cubic))
                h = 0.5 * v
                more = 1.0 + t
                out_v[o] = (h * more).astype(BF)
                grad = more * (0.5 + (h * (ROOT + 3.0 * cubic)) * (1.0 - t))
                slope = (cot_v[o].astype(F32) * grad).astype(BF)
                slope_v[o] = slope
                slopes[g].append(slope)
        part = project(slopes, pair)
        total = part if total is None else total + part
    put(2, total)

    exchange(2)

    gacc[...] = jnp.zeros_like(gacc)

    def outer(at, carry):
        ones = jnp.ones((XB, 2 * N), BF)
        gacc[...] += dot_nt(jnp.concatenate([block_of(field_v, at), ones], axis=0), block_of(slope_v, at))
        return carry

    lax.fori_loop(0, N // (2 * XB), outer, 0)
    same = lax.rem(lax.broadcasted_iota(jnp.int32, (512, 512), 0), XB) == lax.rem(
        lax.broadcasted_iota(jnp.int32, (512, 512), 1), XB
    )
    rows = jnp.sum(jnp.where(same, gacc[: C * XB], 0.0).reshape(C, XB, 512), axis=1)
    bias_rows = gacc[C * XB : C * XB + XB]
    high, low = split(jnp.concatenate([rows, bias_rows], axis=0))
    rows = dot(high, tab["lanes"][...]) + dot(low, tab["lanes"][...])
    lane = lax.broadcasted_iota(jnp.int32, (8, 128), 1) // 32
    packed = jnp.zeros((8, 128), F32)
    for part in range(4):
        packed = packed + jnp.where(lane == part, rows[part * 8 : (part + 1) * 8], 0.0)
    near = x * 2 + core
    sums[0, near, :8] = packed
    sums[0, near, 8:] = rows[C : C + 8]
    peers = [lax.rem(near + at, 8) for at in range(1, 8)]
    share_sums(0, near, [{"slab": peer // 2 * 16 + z * 2 + lax.rem(peer, 2)} for peer in peers])
    pointwise(kl_b, slope_v)
    wait_share(call, 0)
    lax.fori_loop(1, n_ens, spread_member, 0)
    wait_sums(0, 8, sum_recv)
    sums[1, z] = jnp.sum(sums[0], axis=0)
    share_sums(1, z, [{"slab": x * 16 + lax.rem(z + at, 8) * 2 + core} for at in range(1, 8)])

    wait_all(recv, recv_sem, 2)
    back = owned(2)
    ball[mine] = back
    share(ball.at[mine], ball.at[mine], 1)

    four = None
    for g in range(4):
        tall = jnp.concatenate([back[:, g * 128 : (g + 1) * 128]] * 16, axis=0)
        part = dot(jnp.where(own, tall, 0.0).astype(BF), tab["from_modes"][g, :128])
        four = part if four is None else four + part
    four = jnp.concatenate([four, four], axis=1)
    tall = jnp.concatenate([(weights_all(g) * four).astype(BF) for g in range(4)], axis=0)
    tall = dot(tall, tab["gather"][...])
    back_modes = jnp.concatenate([fold_all(tall[g * 512 : (g + 1) * 512], own) for g in range(4)], axis=1)
    planes_out(3, back_modes)
    exchange(3)


    wait_sums(1, 8, sum_recv)
    sums[2, mine] = jnp.sum(sums[1], axis=0)
    share_sums(2, mine, [{"ens": lax.rem(mine + at, n_ens)} for at in range(1, n_ens)])
    wait_share(ball, 1)

    def spectral(chunk, carry):
        keep = own_pair(chunk, 128)
        rows = pl.ds(pl.multiple_of(chunk * 128, 128), 128)
        fours = []
        for member in range(n_ens):
            four = to_channels(ball[member], keep)
            fours.append(jnp.concatenate([four, four], axis=1))
        for g in range(4):
            total = None
            for member in range(n_ens):
                part = cexp[member, rows, g * 256 : (g + 1) * 256] * fours[member]
                total = part if total is None else total + part
            gs_v[pl.ds(chunk * 4, 4), :, g * 256 : (g + 1) * 256] = total.reshape(4, 32, 256)
        return carry

    lax.fori_loop(0, 4, spectral, 0)

    wait_all(recv, recv_sem, 3)
    for g in range(4):
        s2[g * 128 : (g + 1) * 128] = narrow(3, g).astype(BF)
    wait_sums(2, n_ens, sum_recv)
    total_out[...] = sums[2, 0] + sums[2, 1] + sums[2, 2] + sums[2, 3]

    for phase in range(4):
        wait_all(send, send_sem, phase)
    for stage, size in enumerate((8, 8, n_ens)):
        wait_sums(stage, size, sum_send)
    wait_share_sent(call, 0)
    wait_share_sent(ball, 1)


def finish_kernel(out_v, gs_v, pre, s2, total, wide, out, gf, gs, gl, gb, gf_v, gl_v, gb_v, sems):
    stores = []
    for part in range(4):
        eight, four = pl.ds(part * 8, 8), pl.ds(part * 4, 4)
        stores.append(pltpu.make_async_copy(gs_v.at[four], gs.at[four], sems.at[part]))
        stores.append(pltpu.make_async_copy(out_v.at[eight], out.at[eight], sems.at[4 + part]))
    for part in range(4):
        gl_v[part * 8 : (part + 1) * 8, :] = total[:8, part * 32 : (part + 1) * 32]
    gb_v[...] = total[8:9, :32]
    stores.append(pltpu.make_async_copy(gl_v, gl, sems.at[24]))
    stores.append(pltpu.make_async_copy(gb_v, gb, sems.at[25]))
    for store in stores:
        store.start()
    for pair in range(4):
        both = dot(s2[...], wide[:, pair * 256 : (pair + 1) * 256])
        for g in range(4):
            some = pl.ds(g * 8 + pair * 2, 2)
            for half in range(2):
                o = g * 8 + pair * 2 + half
                value = both[g * 128 : (g + 1) * 128, half * 128 : (half + 1) * 128]
                gf_v[o] = (value + pre[o]).astype(BF)
            stores.append(pltpu.make_async_copy(gf_v.at[some], gf.at[some], sems.at[8 + pair * 4 + g]))
            stores[-1].start()
    for store in stores:
        store.wait()


def coefs_at(ref, member, g):
    return ref[member, :, g * 128 : (g + 1) * 128]


def wait_all(ref, sem, phase):
    some = ref.at[phase, pl.ds(0, NZ - 1)]
    pltpu.make_async_copy(some, some, sem.at[phase]).wait()


def local(n_slab, n_ens, field, weight, local_weight, bias, cotangent):
    consts = [jnp.asarray(TABLES[name]) for name in NAMES]
    any_spec = pl.BlockSpec(memory_space=pl.ANY)
    vmem = pl.BlockSpec(memory_space=pltpu.VMEM)
    image = (C, N, N)
    dma = pltpu.SemaphoreType.DMA
    held = pl.pallas_call(
        functools.partial(kernel, n_slab, n_ens),
        out_shape=(
            pltpu.VMEM(image, BF),
            pltpu.VMEM((16, 32, 1024), F32),
            pltpu.VMEM(image, F32),
            pltpu.VMEM((512, 256), BF),
            pltpu.VMEM((16, 128), F32),
        ),
        in_specs=[any_spec] * 5 + [any_spec] * len(NAMES),
        out_specs=(vmem,) * 5,
        scratch_shapes=[pltpu.VMEM(TABLES[name].shape, BF) for name in NAMES]
        + [
            pltpu.VMEM(image, BF),
            pltpu.VMEM(image, BF),
            pltpu.VMEM((16, 32, 1024), BF),
            pltpu.VMEM((32, 32), BF),
            pltpu.SMEM((32,), F32),
            pltpu.VMEM(image, BF),
            pltpu.VMEM((512, 512), BF),
            pltpu.VMEM((512, 512), BF),
            pltpu.VMEM((n_ens, 512, 1024), F32),
            pltpu.VMEM((512 + XB, 512), F32),
            pltpu.VMEM((4, NZ, 4, 128), F32),
            pltpu.VMEM((4, NZ, 4, 128), F32),
            pltpu.VMEM((n_ens, K, 512), F32),
            pltpu.VMEM((n_ens, K, 512), F32),
            pltpu.VMEM((3, 8, 16, 128), F32),
            dma((5,)),
            dma((len(NAMES),)),
            dma((4,)),
            dma((4,)),
            dma((2,)),
            dma((2,)),
            dma((3,)),
            dma((3,)),
        ],
        compiler_params=pltpu.CompilerParams(
            collective_id=0, has_side_effects=True, vmem_limit_bytes=57 * 1024 * 1024
        ),
    )(
        field.reshape(image),
        weight,
        local_weight,
        bias,
        cotangent.reshape(image),
        *consts,
    )
    held = [pltpu.with_memory_space_constraint(value, pltpu.VMEM) for value in (*held, jnp.asarray(WIDE))]
    output, grad_field, grad_spectral, grad_local, grad_bias = pl.pallas_call(
        finish_kernel,
        out_shape=(
            jax.ShapeDtypeStruct(image, BF),
            jax.ShapeDtypeStruct(image, BF),
            jax.ShapeDtypeStruct((16, 32, 1024), F32),
            jax.ShapeDtypeStruct((32, 32), F32),
            jax.ShapeDtypeStruct((1, 32), F32),
        ),
        in_specs=[vmem] * 6,
        out_specs=(any_spec,) * 5,
        scratch_shapes=[pltpu.VMEM(image, BF), pltpu.VMEM((32, 32), F32), pltpu.VMEM((1, 32), F32), dma((26,))],
        compiler_params=pltpu.CompilerParams(vmem_limit_bytes=16 * 1024 * 1024),
    )(*held)
    whole = (1, 1) + image
    return (
        output.reshape(whole),
        grad_field.reshape(whole),
        grad_spectral,
        grad_local,
        grad_bias.reshape(32),
    )


def solution(mesh):
    placed = (
        P("ens", "slab", None, None, None),
        P("slab", None, None),
        P(),
        P(),
        P("ens", "slab", None, None, None),
    )
    return jax.shard_map(
        functools.partial(local, mesh.shape["slab"], mesh.shape["ens"]),
        mesh=mesh,
        in_specs=placed,
        out_specs=(
            P("ens", "slab", None, None, None),
            P("ens", "slab", None, None, None),
            P("slab", None, None),
            P(),
            P(),
        ),
        check_vma=False,
    )
```
